32 devices in a mesh: batch: 2 (over core), seq: 16 (over z, y, x).
Axes of the slice: x: 2, y: 2, z: 4, core: 2. Of those that a mesh axis runs over, the one named last changes fastest.
Arguments:
- token_ids: int32 [2, 4096], P('batch', 'seq'), may hold values from 0 to 3
- complement: int32 [4], replicated, may hold values from 0 to 3, each once
- embedding: bfloat16 [4, 1024], replicated, may hold values from -6 to 6
- in_weight: bfloat16 [1024, 2176], replicated, may hold values from -0.1875 to 0.1875
- step_weight: bfloat16 [1024, 16], replicated, may hold values from -0.1875 to 0.1875
- conv_weight: float32 [2, 4, 1152], replicated, may hold values from -3 to 3
- conv_bias: float32 [2, 1152], replicated, may hold values from -3 to 3
- step_bias: float32 [2, 16], replicated, may hold values from -4 to -2
- decay_rate: float32 [2, 16], replicated, as said below
- skip_gain: float32 [2, 16], replicated, may hold values from 0.5 to 1.5
- norm_gain: float32 [2, 1024], replicated, may hold values from 0.1 to 1.9
- out_weight: bfloat16 [1024, 1024], P('seq', 'batch'), may hold values from -0.1875 to 0.1875
Outputs:
- mixer_output: bfloat16 [2, 4096, 1024], P('batch', 'seq')
The draws below stay inside these ranges and needn't reach their ends.
Inputs may be any that keep to these rules, and one draw needn't show every extreme that they name: `decay_rate`: positive decay rate of each head.
All inputs are finite; a program needn't handle non-finite values.
Results may differ from the reference program's by a relative error of at most 0.0084.
Values may be sent and summed in bfloat16 or wider, within the bound.
No kernel may reach another device: no remote copies, remote signals or barrier semaphores. Data moves between devices by JAX's collectives and lax.ppermute only.
A program may use at most 192 MiB of HBM per device.

```python
import jax
import jax.numpy as jnp
from jax import lax

D = 1024
E = 1024
H = 16
HEADDIM = 64
N = 64
KCONV = 4
BLOCK = 256
GEN = 2
SEQ_LEN = 4096
CONVCH = 1152


def draw_decay_rate(key, part):
    key_slow, key_fast, key_order = jax.random.split(jax.random.fold_in(key, 7), 3)
    slow_rates = jnp.exp(jax.random.uniform(key_slow, (2, H), jnp.float32, jnp.log(3.0), jnp.log(20.0))) / SEQ_LEN
    fast_rates = jnp.exp(jax.random.uniform(key_fast, (2, H), jnp.float32, jnp.log(0.2), jnp.log(1.0)))
    ranks = jnp.stack([jax.random.permutation(jax.random.fold_in(key_order, 0), H), jax.random.permutation(jax.random.fold_in(key_order, 1), H)])
    keep_count = H // 2
    return jnp.where(ranks < keep_count, slow_rates, fast_rates).astype(jnp.float32)


def place_ends(array, rng, least, largest):
    place = [jax.random.randint(jax.random.fold_in(rng, axis), (), 0, length) for axis, length in enumerate(array.shape)]
    main_axis = array.shape.index(max(array.shape))
    next_to = place[:main_axis] + [(place[main_axis] + 1) % array.shape[main_axis]] + place[main_axis + 1:]
    return array.at[tuple(place)].set(least).at[tuple(next_to)].set(largest)


def shard_levels(key, dims, cuts, low, high):
    factor_of = 1.0
    for dim, parts in cuts:
        draws = jax.random.uniform(jax.random.fold_in(jax.random.fold_in(key, 6), dim), (parts,), jnp.float32, low / len(cuts), high / len(cuts))
        factor_of = factor_of * jnp.repeat(jnp.exp(draws), dims[dim] // parts).reshape((-1,) + (1,) * (len(dims) - 1 - dim))
    return factor_of


def noise(rng, extent, deviation, most, pieces=(), dtype=jnp.bfloat16):
    array = jax.random.normal(rng, extent, jnp.float32) * deviation
    if len(pieces) > 0:
        array = shard_levels(rng, extent, pieces, -0.22, 0.18) * array
    return jnp.clip(array, min=-most, max=most).astype(dtype)


def setup_inputs(seed: int = 0) -> dict:
    splits = jax.random.split(jax.random.key(seed), 13)
    return {
        "token_ids": place_ends(jax.random.randint(splits[0], (GEN, SEQ_LEN), 0, 4), jax.random.fold_in(splits[0], 1), 0, 3).astype(jnp.int32),
        "complement": jax.random.permutation(splits[1], 4).astype(jnp.int32),
        "embedding": noise(splits[2], (4, D), 1.0, 6.0),
        "in_weight": noise(splits[3], (D, E + CONVCH), D ** -0.5, 0.1875),
        "step_weight": noise(splits[4], (D, H), D ** -0.5, 0.1875),
        "conv_weight": noise(splits[5], (2, KCONV, CONVCH), KCONV ** -0.5, 3.0, (), jnp.float32),
        "conv_bias": noise(splits[6], (2, CONVCH), 0.5, 3.0, (), jnp.float32),
        "step_bias": jnp.clip(jax.random.uniform(splits[7], (2, H), jnp.float32, -4.0, -2.0), -4.0, -2.0),
        "decay_rate": draw_decay_rate(jax.random.fold_in(splits[12], 71), 0),
        "skip_gain": jnp.clip(jax.random.uniform(splits[9], (2, H), jnp.float32, 0.5, 1.5), 0.5, 1.5),
        "norm_gain": jnp.clip(1.0 + 0.18 * jax.random.normal(splits[10], (2, E), jnp.float32), 0.1, 1.9),
        "out_weight": noise(splits[11], (E, D), E ** -0.5, 0.1875, ((0, 16), (1, 2))),
    }


exact_mode = lax.Precision.HIGHEST
norm_epsilon = 1e-05

def block_step(carry_state, inputs):
    values, b_rows, c_rows, step_sizes, decays = inputs
    running = jnp.cumsum(decays, axis=1)
    spread = running[:, :, None] - running[:, None, :]
    positions = jnp.arange(running.shape[1])
    lower_mask = positions[:, None] >= positions[None, :]
    weights = jnp.exp(jnp.where(lower_mask[None], spread, -jnp.inf))
    scores = jnp.dot(c_rows.astype(jnp.bfloat16), b_rows.astype(jnp.bfloat16).T, preferred_element_type=jnp.float32)
    mixing = weights * scores[None] * step_sizes[:, None, :]
    inside = jnp.einsum('hts,shp->thp', mixing, values, precision=exact_mode)
    carried = jnp.einsum('tn,hpn->thp', c_rows, carry_state, precision=exact_mode)
    carried = carried * jnp.exp(running).T[:, :, None]
    to_end = jnp.exp(running[:, -1:] - running) * step_sizes
    fresh_state = jnp.einsum('hs,shp,sn->hpn', to_end, values, b_rows, precision=exact_mode)
    carry_state = carry_state * jnp.exp(running[:, -1])[:, None, None] + fresh_state
    return (carry_state, inside + carried)

def state_scan(values, b_rows, c_rows, step_sizes, decays, block_rows):
    length, head_count, head_width = values.shape
    block_count = length // block_rows
    blocks = (values.reshape(block_count, block_rows, head_count, head_width), b_rows.reshape(block_count, block_rows, -1), c_rows.reshape(block_count, block_rows, -1), step_sizes.reshape(block_count, block_rows, head_count).transpose(0, 2, 1), decays.reshape(block_count, block_rows, head_count).transpose(0, 2, 1))
    start_state = jnp.zeros((head_count, head_width, b_rows.shape[1]), jnp.float32)
    final_state, outputs = lax.scan(block_step, start_state, blocks)
    return (final_state, outputs.reshape(length, head_count, head_width))

def conv_rows(conv_input, weight_rows, bias_row):
    kernel = weight_rows.shape[0]
    length = conv_input.shape[0]
    padded = jnp.pad(conv_input, ((kernel - 1, 0), (0, 0)))
    conv_total = bias_row[None, :]
    for offset in range(kernel):
        conv_total = conv_total + weight_rows[offset][None, :] * padded[offset:offset + length].astype(jnp.float32)
    return jax.nn.silu(conv_total).astype(jnp.bfloat16)

def gated_norm(outputs, gate_rows, gain_row):
    gated = outputs * jax.nn.silu(gate_rows.astype(jnp.float32))
    scale = lax.rsqrt(lax.optimization_barrier(jnp.mean(gated * gated, axis=-1, keepdims=True)) + norm_epsilon)
    return gated * scale * gain_row[None, :]

def reference(token_ids, complement, embedding, in_weight, step_weight, conv_weight, conv_bias, step_bias, decay_rate, skip_gain, norm_gain, out_weight):

    def direction(conv_input, gate_rows, step_raw, set_index, falling):
        length = conv_input.shape[0]
        if falling:
            conv_input = conv_input[::-1]
            step_raw = step_raw[::-1]
        conved = conv_rows(conv_input, conv_weight[set_index], conv_bias[set_index])
        values = conved[:, :E].astype(jnp.float32).reshape(length, H, HEADDIM)
        b_rows = conved[:, E:E + N].astype(jnp.float32)
        c_rows = conved[:, E + N:].astype(jnp.float32)
        step_sizes = jax.nn.softplus(step_raw + step_bias[set_index][None, :])
        decays = -decay_rate[set_index][None, :] * step_sizes
        final_state, outputs = state_scan(values, b_rows, c_rows, step_sizes, decays, BLOCK)
        outputs = outputs + skip_gain[set_index][None, :, None] * values
        outputs = outputs.reshape(length, E)
        if falling:
            outputs = outputs[::-1]
        return gated_norm(outputs, gate_rows, norm_gain[set_index])

    def strand(strand_rows):
        projected = jnp.dot(strand_rows, in_weight, preferred_element_type=jnp.float32).astype(jnp.bfloat16)
        gate_rows = projected[:, :E]
        conv_input = projected[:, E:]
        step_raw = jnp.dot(strand_rows, step_weight, preferred_element_type=jnp.float32)
        rising = direction(conv_input, gate_rows, step_raw, 0, False)
        falling = direction(conv_input, gate_rows, step_raw, 1, True)
        mixed_rows = (rising + falling).astype(jnp.bfloat16)
        return jnp.dot(mixed_rows, out_weight, preferred_element_type=jnp.float32).astype(jnp.bfloat16)

    def one_genome(tokens):
        flipped = complement[tokens[::-1]]
        forward_out = strand(embedding[tokens])
        other_out = strand(embedding[flipped])
        return (forward_out.astype(jnp.float32) + other_out[::-1].astype(jnp.float32)).astype(jnp.bfloat16)
    return lax.map(one_genome, token_ids)
```

```python
from functools import partial

import jax
import jax.numpy as jnp
import ml_dtypes
import numpy as np
from jax import lax
from jax.experimental import pallas as pl
from jax.experimental.pallas import tpu as pltpu
from jax.sharding import PartitionSpec as P

BLOCK = 256
CHUNK = 64
LANES = 128
WIDE = 256
LOG2E = 1.4426950408889634
EPSILON = 1e-05
F32 = jnp.float32
BF16 = jnp.bfloat16

TN = (((0,), (0,)), ((), ()))
NT = (((1,), (1,)), ((), ()))
NN = (((1,), (0,)), ((), ()))


def dot(a, b, dims=NN):
    return lax.dot_general(a, b, dims, preferred_element_type=F32)


def iota(shape, dim):
    return lax.broadcasted_iota(jnp.int32, shape, dim)


def split3(x):
    high = x.astype(BF16)
    rest = x - high.astype(F32)
    middle = rest.astype(BF16)
    low = (rest - middle.astype(F32)).astype(BF16)
    return high, middle, low


def silu(x):
    return x / (1.0 + jnp.exp(-x))


def word_plan(letters, taps):
    starts = {taps: 0}
    rows = letters**taps
    for length in range(taps - 1, 0, -1):
        starts[length] = rows
        rows += letters**length
    return starts, rows, -(-rows // 32) * 32


def word_letters(letters, taps):
    starts, rows, padded = word_plan(letters, taps)
    table = np.full((padded, taps), -1, np.int64)
    for length, start in starts.items():
        codes = np.arange(letters**length)
        for back in range(length):
            table[start : start + letters**length, taps - 1 - back] = codes // letters**back % letters
    return table


def word_select(letters, taps):
    table = word_letters(letters, taps)
    part = -(-letters * taps // 16) * 16
    select = np.zeros((table.shape[0], 4 * part), np.float32)
    for tap in range(taps):
        rows = np.nonzero(table[:, tap] >= 0)[0]
        for copy in range(3):
            select[rows, copy * part + tap * letters + table[rows, tap]] = 1
    select[:, 3 * part : 3 * part + 3] = 1
    last = np.zeros((table.shape[0], 32), np.float32)
    rows = np.nonzero(table[:, taps - 1] >= 0)[0]
    for copy in range(2):
        last[rows, copy * 16 + table[rows, taps - 1]] = 1
    return select.astype(ml_dtypes.bfloat16), last.astype(ml_dtypes.bfloat16)


PASSES = ((False, 0, 0), (False, 1, 1), (True, 0, 1), (True, 1, 0))


def letter_rows(table, letters, rows, complement):
    row = iota((rows, 1), 0) % letters
    picked = row
    if complement is not None:
        picked = jnp.zeros_like(row)
        for letter in range(letters):
            picked = jnp.where(row == letter, complement(letter), picked)
    result = jnp.broadcast_to(table[0:1], (rows, table.shape[1]))
    for letter in range(1, letters):
        result = jnp.where(picked == letter, table[letter : letter + 1], result)
    return result


def pack_split(x, copies):
    return jnp.concatenate(split3(x)[:copies], axis=0)


def tables_kernel(
    complement_ref,
    embedding_ref,
    in_weight_ref,
    step_weight_ref,
    conv_weight_ref,
    conv_bias_ref,
    step_bias_ref,
    rate_ref,
    skip_ref,
    select_ref,
    last_ref,
    spread_ref,
    words_ref,
    stepped_ref,
    gates_ref,
    decay_ref,
    log_step_ref,
    skip_out_ref,
    narrow_decay_ref,
    narrow_step_ref,
    tall_decay_ref,
):
    letters, width = embedding_ref.shape
    taps = conv_weight_ref.shape[1]
    heads = step_weight_ref.shape[1]
    inner = spread_ref.shape[1]
    state = (conv_weight_ref.shape[2] - inner) // 2
    part = select_ref.shape[1] // 4
    embedding = jnp.concatenate(
        [embedding_ref[...], jnp.zeros((16 - letters, width), BF16)], axis=0
    )
    projected = dot(embedding, in_weight_ref[...]).astype(BF16).astype(F32)
    raw = dot(embedding, step_weight_ref[...])
    complement = lambda letter: complement_ref[letter]
    spread = spread_ref[...]

    def widen(x):
        return sum(dot(piece, spread) for piece in split3(x))

    row = iota((16, heads), 0)
    vectors = jnp.zeros((16, heads), F32)
    for index in range(2):
        vectors = jnp.where(row == index, step_bias_ref[index : index + 1, :], vectors)
        vectors = jnp.where(row == 2 + index, rate_ref[index : index + 1, :], vectors)
        vectors = jnp.where(row == 4 + index, skip_ref[index : index + 1, :], vectors)
    wide_vectors = widen(vectors)
    wide_raw = widen(raw)

    def step_tables(raw_rows, vector_rows, strand, param):
        rows = letter_rows(raw_rows, letters, 8, complement if strand else None)
        shifted = rows + vector_rows[param : param + 1]
        step = jnp.maximum(shifted, 0.0) + jnp.log1p(jnp.exp(-jnp.abs(shifted)))
        decay = -vector_rows[2 + param : 3 + param] * step * LOG2E
        return step, decay, jnp.log2(step)

    gate = silu(projected[:, :inner])
    for strand in range(2):
        rows = letter_rows(gate, letters, 16, complement if strand else None)
        rows = jnp.where(iota((16, 1), 0) < letters, rows, 0.0)
        gates_ref[strand] = pack_split(rows, 2)

    for index, (falls, strand, param) in enumerate(PASSES):
        step, decay, log_step = step_tables(wide_raw, wide_vectors, strand, param)
        decay_ref[index] = decay
        log_step_ref[index] = log_step
        skip_out_ref[index] = jnp.broadcast_to(wide_vectors[4 + param : 5 + param], (8, inner))
        narrow_step, narrow_decay, narrow_log = step_tables(raw, vectors, strand, param)
        narrow_decay_ref[index] = narrow_decay
        narrow_step_ref[index] = narrow_log
        square = jnp.concatenate([narrow_decay, jnp.zeros((8, LANES - heads), F32)], axis=1)
        square = jnp.concatenate([square, jnp.zeros((LANES - 8, LANES), F32)], axis=0)
        tall_decay_ref[index] = square.T[:heads]

        inputs = letter_rows(projected[:, inner:], letters, part, complement if strand else None)
        tap_row = iota((part, 1), 0) // letters
        weights = jnp.zeros((part, inputs.shape[1]), F32)
        for tap in range(taps):
            weights = jnp.where(tap_row == tap, conv_weight_ref[param, tap : tap + 1, :], weights)
        bias = conv_bias_ref[param : param + 1, :]
        bias_rows = jnp.zeros((part, inputs.shape[1]), F32)
        for place, piece in enumerate(split3(bias)):
            bias_rows = jnp.where(iota((part, 1), 0) == place, piece.astype(F32), bias_rows)
        products = jnp.concatenate([*split3(weights * inputs), bias_rows.astype(BF16)], axis=0)
        conved = silu(dot(select_ref[...], products))
        values = conved[:, :inner].astype(BF16)
        rest = conved[:, inner:]
        lane = iota(rest.shape, 1)
        words_ref[index, :, :inner] = values
        words_ref[index, :, inner : inner + LANES] = jnp.where(lane < state, rest, 0.0).astype(BF16)
        words_ref[index, :, inner + LANES :] = jnp.where(
            lane < state, pltpu.roll(rest, LANES - state, 1), 0.0
        ).astype(BF16)
        step_rows = jnp.concatenate([step, jnp.zeros((8, inner), F32)], axis=0)
        word_steps = dot(last_ref[...], pack_split(step_rows, 2))
        stepped_ref[index] = (values.astype(F32) * word_steps).astype(BF16)


def mixer_kernel(
    letters,
    taps,
    state,
    here_ref,
    tokens_ref,
    words_ref,
    stepped_ref,
    gates_ref,
    decay_ref,
    log_step_ref,
    skip_ref,
    narrow_decay_ref,
    narrow_step_ref,
    tall_decay_ref,
    gain_ref,
    spread_ref,
    mixed_ref,
    state_ref,
    conved_ref,
    total_ref,
):
    here = here_ref[0]
    blocks = tokens_ref.shape[0]
    rows = mixed_ref.shape[0]
    own = rows // BLOCK
    heads, inner = spread_ref.shape
    head = inner // heads
    word_rows = words_ref.shape[1]
    starts, _, _ = word_plan(letters, taps)
    first, past = here * own, (here + 1) * own

    place = iota((blocks, blocks), 1)
    place = (here ^ (place // own)) * own + place % own
    target = iota((blocks, blocks), 0)
    tokens = tokens_ref[...].astype(F32).astype(BF16)
    around = []
    for offset in (-1, 0, 1):
        pick = (place == target + offset).astype(F32).astype(BF16)
        around.append(dot(pick, tokens))
    before, middle, after = (x.astype(jnp.int32) for x in around)
    position = iota((blocks, BLOCK), 0) * BLOCK + iota((blocks, BLOCK), 1)

    def word_index(both, shifts, at_end):
        codes = jnp.zeros((blocks, BLOCK), jnp.int32)
        result = None
        scale = 1
        for back in range(taps):
            start = BLOCK if shifts > 0 else 0
            turned = both if back == 0 else pltpu.roll(both, back if shifts > 0 else 2 * BLOCK - back, 1)
            codes = codes + scale * turned[:, start : start + BLOCK]
            scale *= letters
            found = starts[back + 1] + codes
            result = found if result is None else jnp.where(at_end >= back, found, result)
        return result

    rise_index = word_index(jnp.concatenate([before, middle], axis=1), 1, position)
    fall_index = word_index(
        jnp.concatenate([middle, after], axis=1), -1, blocks * BLOCK - 1 - position
    )

    hot = [(middle == letter).astype(F32) for letter in range(letters)]
    stack = jnp.concatenate(hot, axis=0).astype(BF16)
    up = (iota((BLOCK, BLOCK), 0) <= iota((BLOCK, BLOCK), 1)).astype(F32).astype(BF16)
    running = dot(stack, up)
    block_sum = dot(stack, jnp.ones((BLOCK, BLOCK), BF16)).astype(BF16)
    col = iota((blocks, blocks), 1)
    to_rise = ((col >= target) & (col < first)).astype(F32).astype(BF16)
    to_fall = ((col >= past) & (col < target)).astype(F32).astype(BF16)
    block_of = iota((blocks, BLOCK), 0)
    counts = []
    for letter in range(letters):
        part = slice(letter * blocks, (letter + 1) * blocks)
        rise = dot(to_rise, block_sum[part]) - running[part]
        fall = dot(to_fall, block_sum[part]) + running[part] - hot[letter]
        counts.append(jnp.where(block_of < first, rise, fall))
    index = jnp.where(block_of < first, rise_index, fall_index)

    rise_tall = jnp.concatenate([tall_decay_ref[0], tall_decay_ref[1]], axis=0)
    fall_tall = jnp.concatenate([tall_decay_ref[2], tall_decay_ref[3]], axis=0)
    word = iota((word_rows, BLOCK), 0)
    word_weights = jnp.zeros((word_rows, 4 * heads), F32)
    for block in range(blocks):
        rises, falls = block < first, block >= past
        tall = jnp.where(rises, rise_tall, fall_tall)
        power = sum(counts[l][block : block + 1] * tall[:, l : l + 1] for l in range(letters))
        weight = jnp.exp2(power)
        both = jnp.concatenate(
            [jnp.where(rises, weight, 0.0), jnp.where(falls, weight, 0.0)], axis=0
        ).astype(BF16)
        match = (word == index[block : block + 1]).astype(F32).astype(BF16)
        word_weights = word_weights + dot(match, both, NT)
    word_weights = word_weights.astype(BF16)
    spread = spread_ref[...]
    pass_of = iota((4 * heads, inner), 0) // heads
    spread4 = jnp.concatenate([spread] * 4, axis=0)
    for index4 in range(4):
        spread_one = jnp.where(pass_of == index4, spread4.astype(F32), 0.0).astype(BF16)
        weighted = (dot(word_weights, spread_one) * stepped_ref[index4].astype(F32)).astype(BF16)
        entering = dot(words_ref[index4, :, inner : inner + LANES], weighted, TN)
        state_ref[index4] = entering[:state]

    own_tokens, own_match = [], []
    for part in range(own):
        is_row = block_of == first + part
        take = lambda x: jnp.sum(jnp.where(is_row, x, 0), axis=0, keepdims=True)
        own_tokens.append(take(middle))
        pair = []
        for found in (rise_index, fall_index):
            pair.append((word == take(found)).astype(F32).astype(BF16))
        own_match.append(pair)
    for part in range(own):
        for index4, (falls, strand, param) in enumerate(PASSES):
            conved_ref[index4, part * BLOCK : (part + 1) * BLOCK, :] = dot(
                own_match[part][int(falls)], words_ref[index4], TN
            ).astype(BF16)

    per_block = BLOCK // CHUNK
    chunks = rows // CHUNK
    t = iota((CHUNK, LANES), 0)
    lane = iota((CHUNK, LANES), 1)
    half = lane % CHUNK
    u_row = iota((LANES, LANES), 0)
    u_half = iota((LANES, LANES), 1) % CHUNK
    lane_row = iota((1, LANES), 1)

    def window(chunk):
        block, inside = chunk // per_block, chunk % per_block
        pair = inside // 2
        side = inside % 2
        return own_tokens[block][:, pair * LANES : (pair + 1) * LANES], side * CHUNK

    def letter_counts(chunk, falls):
        tokens_row, base = window(chunk)
        u = lane - base
        in_chunk = (u >= 0) & (u < CHUNK)
        reach = in_chunk & ((u >= t) if falls else (u <= t))
        left = jnp.concatenate(
            [jnp.where(reach & (tokens_row == l), 1.0, 0.0) for l in range(letters)], axis=0
        ).astype(BF16)
        v = u_row - base
        beyond = (v < u_half) if falls else (v > u_half)
        right = jnp.concatenate(
            [jnp.where(beyond, 1.0, 0.0), jnp.ones((LANES, LANES), F32)], axis=1
        ).astype(BF16)
        both = dot(left, right)
        between = [both[l * CHUNK : (l + 1) * CHUNK, :LANES] for l in range(letters)]
        running = [both[l * CHUNK : (l + 1) * CHUNK, LANES:] for l in range(letters)]
        return between, running

    for step in range(chunks):
        for falls in (False, True):
            chunk = chunks - 1 - step if falls else step
            at = slice(chunk * CHUNK, (chunk + 1) * CHUNK)
            between, running = letter_counts(chunk, falls)
            _, other = letter_counts(chunk, not falls)
            edge = 0 if falls else CHUNK - 1
            sums = [r[edge : edge + 1] for r in running]
            is_letter = [r + o - s for r, o, s in zip(running, other, sums)]
            tokens_row, base = window(chunk)
            turned = pltpu.roll(tokens_row, CHUNK, 1)
            doubled = jnp.where((lane_row >= base) & (lane_row < base + CHUNK), tokens_row, turned)
            hot_cols = jnp.zeros((CHUNK, LANES), F32)
            for l in range(letters):
                hot_cols = jnp.where((lane == l) | (lane == 16 + l), is_letter[l], hot_cols)
            hot_cols = hot_cols[:, :32].astype(BF16)
            causal = (half >= t) if falls else (half <= t)
            for index4, (pass_falls, strand, param) in enumerate(PASSES):
                if pass_falls != falls:
                    continue
                values = conved_ref[index4, at, :inner]
                b_rows = conved_ref[index4, at, inner : inner + LANES]
                c_rows = conved_ref[index4, at, inner + LANES :]
                scores = dot(c_rows, jnp.concatenate([b_rows, b_rows], axis=0), NT)
                scores = jnp.where(causal, scores, 0.0)
                narrow_decay = narrow_decay_ref[index4]
                narrow_log = narrow_step_ref[index4]
                width = slice(0, heads)
                power = sum(running[l][:, width] * narrow_decay[l : l + 1] for l in range(letters))
                from_start = jnp.exp2(power).astype(BF16)
                power = sum(
                    (sums[l] - running[l])[:, width] * narrow_decay[l : l + 1] for l in range(letters)
                )
                logs = jnp.zeros((CHUNK, heads), F32)
                for l in range(letters):
                    logs = jnp.where(is_letter[l][:, width] > 0.5, narrow_log[l : l + 1], logs)
                to_end = jnp.exp2(power + logs).astype(BF16)
                from_start = dot(from_start, spread)
                to_end = dot(to_end, spread)
                old = state_ref[index4]
                carried = dot(c_rows[:, :state], old.astype(BF16))
                fresh = dot(b_rows, (values.astype(F32) * to_end).astype(BF16), TN)[:state]
                outputs = []
                for group in range(inner // WIDE):
                    mixing = []
                    for tile in range(WIDE // LANES):
                        lanes = slice(
                            group * WIDE + tile * LANES, group * WIDE + (tile + 1) * LANES
                        )
                        power = log_step_ref[index4, 0:1, lanes]
                        for l in range(1, letters):
                            power = jnp.where(
                                doubled == l, log_step_ref[index4, l : l + 1, lanes], power
                            )
                        for l in range(letters):
                            power = power + between[l] * decay_ref[index4, l : l + 1, lanes]
                        mixing.append((jnp.exp2(power) * scores).astype(BF16))
                    mixing = jnp.concatenate(mixing, axis=1)
                    wide = slice(group * WIDE, (group + 1) * WIDE)
                    group_values = values[:, wide]
                    head_of = iota((CHUNK, WIDE), 1) // head
                    stacked = jnp.concatenate(
                        [
                            jnp.where(head_of == h, group_values.astype(F32), 0.0).astype(BF16)
                            for h in range(WIDE // head)
                        ],
                        axis=0,
                    )
                    inside = dot(mixing, stacked)
                    outputs.append(
                        inside
                        + carried[:, wide] * from_start[:, wide]
                        + skip_ref[index4, 0:1, wide] * group_values.astype(F32)
                    )
                total_decay = jnp.zeros((1, inner), F32)
                for l in range(letters):
                    total = jnp.concatenate([sums[l]] * (inner // LANES), axis=1)
                    total_decay = total_decay + total * decay_ref[index4, l : l + 1]
                state_ref[index4] = old * jnp.exp2(total_decay) + fresh
                gated = jnp.concatenate(outputs, axis=1) * dot(hot_cols, gates_ref[strand])
                mean = jnp.sum(gated * gated, axis=1, keepdims=True) * (1.0 / inner)
                normed = gated * lax.rsqrt(mean + EPSILON) * gain_ref[param : param + 1]
                visited = index4 in (1, 3) or 2 * step >= chunks
                if visited:
                    total_ref[at, :] += normed
                else:
                    total_ref[at, :] = normed
    mixed_ref[...] = total_ref[...].astype(BF16)


def output_kernel(masks, sides, here_ref, side_ref, mixed_ref, *refs):
    pieces = refs[: len(masks)]
    out_ref, weight_ref, sem = refs[len(masks) :]
    here, side = here_ref[0], side_ref[0]
    copies = []
    for piece, piece_masks, piece_side in zip(pieces, masks, sides):
        depth, width = piece.shape[1:]
        for k, mask in enumerate(piece_masks):
            row = pl.multiple_of((here ^ mask) * depth, depth)
            lane = pl.multiple_of((side ^ piece_side) * width, width)
            copies.append(
                pltpu.make_async_copy(
                    piece.at[k], weight_ref.at[pl.ds(row, depth), pl.ds(lane, width)], sem
                )
            )
    for copy in copies:
        copy.start()
    for copy in copies:
        copy.wait()
    out_ref[...] = dot(mixed_ref[...], weight_ref[...]).astype(BF16)


def swap(x, axis, mask):
    count = lax.axis_size(axis)
    return lax.ppermute(x, axis, [(i, i ^ mask) for i in range(count)])


def vmem():
    return pl.BlockSpec(memory_space=pltpu.VMEM)


def smem():
    return pl.BlockSpec(memory_space=pltpu.SMEM)


def on_device(
    token_ids,
    complement,
    embedding,
    in_weight,
    step_weight,
    conv_weight,
    conv_bias,
    step_bias,
    decay_rate,
    skip_gain,
    norm_gain,
    out_weight,
):
    genomes, rows = token_ids.shape
    letters, width = embedding.shape
    taps = conv_weight.shape[1]
    heads = step_weight.shape[1]
    inner = norm_gain.shape[1]
    state = (conv_weight.shape[2] - inner) // 2
    count, sides = lax.axis_size("seq"), lax.axis_size("batch")
    here = lax.axis_index("seq").astype(jnp.int32)[None]
    side = lax.axis_index("batch").astype(jnp.int32)[None]
    depth, columns = out_weight.shape

    token_rows = -(-genomes * rows // columns)
    padded_rows = -(-token_rows // 16) * 16
    flat = token_ids.astype(BF16).reshape(-1)
    flat = jnp.pad(flat, (0, padded_rows * columns - flat.shape[0]))
    load = jnp.concatenate([out_weight, flat.reshape(padded_rows, columns)], axis=0)[None]

    line = [mask for mask in range(0, count, 4)]
    lines = jnp.concatenate([load] + [swap(load, "seq", mask) for mask in line[1:]], axis=0)
    half = len(line) // 2
    from_x, from_y = swap(lines, "seq", 1), swap(lines, "seq", 2)
    corner_low = swap(from_y[:half], "seq", 1)
    corner_high = swap(from_x[half:], "seq", 2)
    pieces = [
        (lines, line),
        (from_x, [m ^ 1 for m in line]),
        (from_y, [m ^ 2 for m in line]),
        (corner_low, [m ^ 3 for m in line[:half]]),
        (corner_high, [m ^ 3 for m in line[half:]]),
    ]
    weights = jnp.concatenate([piece for piece, _ in pieces], axis=0)
    masks = [m for _, piece_masks in pieces for m in piece_masks]
    held = [weights[:, :depth]]
    held_sides = [0]
    mask = 1
    while mask < sides:
        held = held + [swap(x, "batch", mask) for x in held]
        held_sides = held_sides + [s ^ mask for s in held_sides]
        mask *= 2

    travelled = weights[:, depth:].reshape(count, -1)[:, : genomes * rows]
    order = np.argsort(masks)
    travelled = jnp.concatenate([travelled[int(k)][None] for k in order], axis=0)
    travelled = travelled.astype(jnp.int32).reshape(count, genomes, rows)

    select, last = word_select(letters, taps)
    word_rows = select.shape[0]
    spread = np.repeat(np.eye(heads, dtype=np.float32), inner // heads, axis=1).astype(
        ml_dtypes.bfloat16
    )
    table_columns = inner + 2 * LANES
    shapes = [
        ((4, word_rows, table_columns), BF16),
        ((4, word_rows, inner), BF16),
        ((2, 32, inner), BF16),
        ((4, 8, inner), F32),
        ((4, 8, inner), F32),
        ((4, 8, inner), F32),
        ((4, 8, heads), F32),
        ((4, 8, heads), F32),
        ((4, heads, LANES), F32),
    ]
    tables = pl.pallas_call(
        tables_kernel,
        out_shape=[jax.ShapeDtypeStruct(*shape) for shape in shapes],
        in_specs=[smem()] + [vmem()] * 11,
        out_specs=[vmem()] * len(shapes),
        compiler_params=pltpu.CompilerParams(vmem_limit_bytes=20 * 2**20),
        cost_estimate=pl.CostEstimate(flops=3 * 10**9, bytes_accessed=16 * 2**20, transcendentals=2**21),
        name="tables",
    )(
        complement,
        embedding,
        in_weight,
        step_weight,
        conv_weight,
        conv_bias,
        step_bias,
        decay_rate,
        skip_gain,
        select,
        last,
        spread,
    )
    results = []
    for genome in range(genomes):
        tokens = travelled[:, genome].reshape(-1, BLOCK)
        mixed = pl.pallas_call(
            partial(mixer_kernel, letters, taps, state),
            out_shape=jax.ShapeDtypeStruct((rows, inner), BF16),
            in_specs=[smem()] + [vmem()] * 12,
            out_specs=vmem(),
            scratch_shapes=[
                pltpu.VMEM((4, state, inner), F32),
                pltpu.VMEM((4, rows, table_columns), BF16),
                pltpu.VMEM((rows, inner), F32),
            ],
            compiler_params=pltpu.CompilerParams(vmem_limit_bytes=20 * 2**20),
            cost_estimate=pl.CostEstimate(
                flops=6 * 10**9, bytes_accessed=24 * 2**20, transcendentals=2**21
            ),
            name="mixer",
        )(here, tokens, *tables, norm_gain, spread)
        result = pl.pallas_call(
            partial(output_kernel, [masks] * len(held), held_sides),
            out_shape=jax.ShapeDtypeStruct((rows, columns * sides), BF16),
            in_specs=[smem(), smem(), vmem()] + [pl.BlockSpec(memory_space=pl.ANY)] * len(held),
            out_specs=vmem(),
            scratch_shapes=[
                pltpu.VMEM((depth * count, columns * sides), BF16),
                pltpu.SemaphoreType.DMA,
            ],
            compiler_params=pltpu.CompilerParams(vmem_limit_bytes=8 * 2**20),
            name="output",
        )(here, side, mixed, *held)
        results.append(result)
    return jnp.stack(results)


def solution(mesh):
    placed = (P("batch", "seq"),) + (P(),) * 10 + (P("seq", "batch"),)
    return jax.shard_map(
        on_device, mesh=mesh, in_specs=placed, out_specs=P("batch", "seq", None), check_vma=False
    )
```

```python
from functools import partial

import jax
import jax.numpy as jnp
import ml_dtypes
import numpy as np
from jax import lax
from jax.experimental import pallas as pl
from jax.experimental.pallas import tpu as pltpu
from jax.sharding import PartitionSpec as P

BLOCK = 256
CHUNK = 64
LANES = 128
WIDE = 256
LOG2E = 1.4426950408889634
EPSILON = 1e-05
VMEM_BYTES = 64 * 2**20
F32 = jnp.float32
BF16 = jnp.bfloat16

TN = (((0,), (0,)), ((), ()))
NT = (((1,), (1,)), ((), ()))
NN = (((1,), (0,)), ((), ()))


def dot(a, b, dims=NN):
    return lax.dot_general(a, b, dims, preferred_element_type=F32)


def iota(shape, dim):
    return lax.broadcasted_iota(jnp.int32, shape, dim)


def split3(x):
    high = x.astype(BF16)
    rest = x - high.astype(F32)
    middle = rest.astype(BF16)
    low = (rest - middle.astype(F32)).astype(BF16)
    return high, middle, low


def silu(x):
    return x / (1.0 + jnp.exp(-x))


def word_plan(letters, taps):
    starts = {taps: 0}
    rows = letters**taps
    for length in range(taps - 1, 0, -1):
        starts[length] = rows
        rows += letters**length
    return starts, rows, -(-rows // 32) * 32


def word_letters(letters, taps):
    starts, rows, padded = word_plan(letters, taps)
    table = np.full((padded, taps), -1, np.int64)
    for length, start in starts.items():
        codes = np.arange(letters**length)
        for back in range(length):
            table[start : start + letters**length, taps - 1 - back] = codes // letters**back % letters
    return table


def word_select(letters, taps):
    table = word_letters(letters, taps)
    part = -(-letters * taps // 16) * 16
    select = np.zeros((table.shape[0], 4 * part), np.float32)
    for tap in range(taps):
        rows = np.nonzero(table[:, tap] >= 0)[0]
        for copy in range(3):
            select[rows, copy * part + tap * letters + table[rows, tap]] = 1
    select[:, 3 * part : 3 * part + 3] = 1
    last = np.zeros((table.shape[0], 32), np.float32)
    rows = np.nonzero(table[:, taps - 1] >= 0)[0]
    for copy in range(2):
        last[rows, copy * 16 + table[rows, taps - 1]] = 1
    return select.astype(ml_dtypes.bfloat16), last.astype(ml_dtypes.bfloat16)


PASSES = ((False, 0, 0), (False, 1, 1), (True, 0, 1), (True, 1, 0))


def letter_rows(table, letters, rows, complement):
    row = iota((rows, 1), 0) % letters
    picked = row
    if complement is not None:
        picked = jnp.zeros_like(row)
        for letter in range(letters):
            picked = jnp.where(row == letter, complement(letter), picked)
    result = jnp.broadcast_to(table[0:1], (rows, table.shape[1]))
    for letter in range(1, letters):
        result = jnp.where(picked == letter, table[letter : letter + 1], result)
    return result


def pack_split(x, copies):
    return jnp.concatenate(split3(x)[:copies], axis=0)


def start_all(pairs, sems):
    copies = [
        pltpu.make_async_copy(source, target, sems.at[k]) for k, (source, target) in enumerate(pairs)
    ]
    for copy in copies:
        copy.start()
    return copies


def word_index(both, start, size, falls, starts, taps, letters, before_end):
    lanes = both.shape[1]
    codes, result, scale = None, None, 1
    for back in range(taps):
        turned = both if back == 0 else pltpu.roll(both, lanes - back if falls else back, 1)
        part = scale * turned[:, start : start + size]
        codes = part if codes is None else codes + part
        scale *= letters
        found = starts[back + 1] + codes
        result = found if result is None else jnp.where(before_end >= back, found, result)
    return result


def spread_rows(spread, index, count):
    heads = spread.shape[0]
    stacked = jnp.concatenate([spread] * count, axis=0)
    return jnp.where(iota(stacked.shape, 0) // heads == index, stacked, jnp.zeros_like(stacked))


def mixer_kernel(
    letters,
    taps,
    state,
    count,
    here_ref,
    complement_ref,
    tokens_hbm,
    spread_hbm,
    embedding_hbm,
    step_weight_hbm,
    step_bias_hbm,
    rate_hbm,
    skip_hbm,
    last_hbm,
    select_hbm,
    conv_weight_hbm,
    conv_bias_hbm,
    gain_hbm,
    in_weight_hbm,
    mixed_hbm,
    tokens_ref,
    spread_ref,
    embedding_ref,
    step_weight_ref,
    step_bias_ref,
    rate_ref,
    skip_ref,
    last_ref,
    select_ref,
    conv_weight_ref,
    conv_bias_ref,
    gain_ref,
    in_weight_ref,
    mixed_ref,
    words_ref,
    gates_ref,
    coefs_ref,
    exponent_ref,
    match_ref,
    weight_ref,
    base_ref,
    gated_ref,
    in_sems,
    out_sem,
):
    reads = start_all(
        (
            (tokens_hbm, tokens_ref),
            (spread_hbm, spread_ref),
            (embedding_hbm, embedding_ref),
            (step_weight_hbm, step_weight_ref),
            (step_bias_hbm, step_bias_ref),
            (rate_hbm, rate_ref),
            (skip_hbm, skip_ref),
            (last_hbm, last_ref),
            (select_hbm, select_ref),
            (conv_weight_hbm, conv_weight_ref),
            (conv_bias_hbm, conv_bias_ref),
            (gain_hbm, gain_ref),
            (in_weight_hbm, in_weight_ref),
        ),
        in_sems,
    )
    here = here_ref[0]
    rows = tokens_ref.shape[1]
    own = rows // BLOCK
    blocks = count * own
    heads, inner = spread_ref.shape
    head = inner // heads
    word_rows = select_ref.shape[0]
    part_rows = select_ref.shape[1] // 4
    starts, _, _ = word_plan(letters, taps)
    first, past = here * own, (here + 1) * own
    chunks = BLOCK // CHUNK
    as_bf16 = lambda mask: jnp.where(mask, 1.0, 0.0).astype(BF16)
    complement = lambda letter: complement_ref[letter]

    reads[0].wait()
    tokens16 = tokens_ref[...].astype(F32).astype(BF16)
    source, target = iota((blocks, count), 1) ^ here, iota((blocks, count), 0)
    around = jnp.zeros((3 * blocks, BLOCK), F32)
    for part in range(own):
        block = source * own + part
        pick = jnp.concatenate([as_bf16(block == target + k) for k in (-1, 0, 1)], axis=0)
        around = around + dot(pick, tokens16[:, part * BLOCK : (part + 1) * BLOCK])
    around = around.astype(jnp.int32)
    before, middle, after = (around[k * blocks : (k + 1) * blocks] for k in range(3))
    position = iota((blocks, BLOCK), 0) * BLOCK + iota((blocks, BLOCK), 1)
    rise_index = word_index(
        jnp.concatenate([before, middle], axis=1), BLOCK, BLOCK, False, starts, taps, letters, position
    )
    fall_index = word_index(
        jnp.concatenate([middle, after], axis=1),
        0,
        BLOCK,
        True,
        starts,
        taps,
        letters,
        blocks * BLOCK - 1 - position,
    )
    block_of = iota((blocks, BLOCK), 0)
    middle_word = word_rows // 2
    word = (iota((word_rows, BLOCK), 0) - middle_word).astype(F32).astype(BF16)
    index = jnp.where(block_of < first, rise_index, fall_index) - middle_word
    index = index.astype(F32).astype(BF16)
    one, zero = jnp.ones((), BF16), jnp.zeros((), BF16)
    for block in range(blocks):
        match_ref[:, block * BLOCK : (block + 1) * BLOCK] = jnp.where(
            word == index[block : block + 1], one, zero
        )

    letter_hot = [jnp.where(middle == letter, 1.0, 0.0) for letter in range(letters)]
    stack = jnp.concatenate(letter_hot, axis=0).astype(BF16)
    t = iota((BLOCK, BLOCK), 0)
    u = iota((BLOCK, BLOCK), 1)
    sums = dot(stack, jnp.concatenate([as_bf16(t <= u), jnp.ones((BLOCK, BLOCK), BF16)], axis=1))
    running, block_sum = sums[:, :BLOCK], sums[:, BLOCK:].astype(BF16)
    col, row = iota((blocks, blocks), 1), iota((blocks, blocks), 0)
    to_rise = as_bf16((col >= row) & (col < first))
    to_fall = as_bf16((col >= past) & (col < row))
    both_ways = jnp.concatenate([to_rise, to_fall], axis=0)
    counts = []
    for letter in range(letters):
        part = slice(letter * blocks, (letter + 1) * blocks)
        far = dot(both_ways, block_sum[part])
        rise = far[:blocks] - running[part]
        fall = far[blocks:] + running[part] - letter_hot[letter]
        counts.append(jnp.where(block_of < first, rise, fall))

    same = (t // CHUNK) == (u // CHUNK)
    until, since = as_bf16(same & (u <= t)), as_bf16(same & (u >= t))
    half = iota((BLOCK, LANES), 1) % CHUNK
    inside_row = iota((BLOCK, LANES), 0) % CHUNK
    lane = iota((BLOCK, LANES), 1)
    hot_lane = jnp.where(lane < 48, (lane % 16).astype(F32), -1.0)
    word_lane = iota((BLOCK, word_rows), 1).astype(F32)
    small_half = iota((CHUNK, LANES), 1) % CHUNK
    small_row = iota((CHUNK, LANES), 0)
    small_lane = iota((CHUNK, LANES), 1)
    row_lane = iota((1, LANES), 1)
    beyond = (as_bf16(inside_row > half), as_bf16(inside_row < half))
    row8 = iota((8, BLOCK), 0)
    prepared = []
    for part in range(own):
        mine = block_of == first + part
        take = lambda x: jnp.sum(jnp.where(mine, x, 0), axis=0, keepdims=True)
        token_row = take(middle).astype(F32)
        facts = jnp.where(row8 == 0, take(rise_index), take(fall_index)).astype(F32)
        facts = jnp.where(row8 == 2, token_row, facts)
        facts = jnp.concatenate([facts, jnp.zeros((LANES - 8, BLOCK), F32)], axis=0).T
        matches = [
            jnp.where(word_lane == facts[:, d : d + 1], 1.0, 0.0).astype(BF16) for d in range(2)
        ]
        hot = jnp.where(hot_lane == facts[:, 2:3], 1.0, 0.0)
        hot16 = hot.astype(BF16)
        tallies = dot(jnp.concatenate([until, since], axis=0), hot16)
        hot_rows = [jnp.where(token_row == l, 1.0, 0.0) for l in range(letters)]
        between = []
        for d, reach in enumerate((until, since)):
            left = jnp.concatenate([reach * h.astype(BF16) for h in hot_rows], axis=0)
            between.append(dot(left, beyond[d]))
        totals = jnp.concatenate(
            [jnp.where(u[:1] // CHUNK == i, h, 0.0) for i in range(chunks) for h in hot_rows],
            axis=0,
        ).astype(BF16)
        totals = dot(totals, jnp.ones((BLOCK, LANES), BF16))
        doubled = []
        for i in range(chunks):
            window = token_row[:, (i // 2) * LANES : (i // 2 + 1) * LANES]
            keep = (row_lane // CHUNK) == i % 2
            doubled.append(jnp.where(keep, window, pltpu.roll(window, CHUNK, 1)))
        prepared.append((matches, hot, hot16, tallies, between, totals, doubled))

    for copy in reads[1:8]:
        copy.wait()
    spread = spread_ref[...]
    width = embedding_ref.shape[1]
    embedding = jnp.concatenate(
        [embedding_ref[...], jnp.zeros((16 - letters, width), BF16)], axis=0
    )
    raw = dot(embedding, step_weight_ref[...], NT)

    def widen(x):
        return sum(dot(piece, spread) for piece in split3(x))

    row = iota((16, heads), 0)
    vectors = jnp.zeros((16, heads), F32)
    for k in range(2):
        vectors = jnp.where(row == k, step_bias_ref[k : k + 1, :], vectors)
        vectors = jnp.where(row == 2 + k, rate_ref[k : k + 1, :], vectors)
        vectors = jnp.where(row == 4 + k, skip_ref[k : k + 1, :], vectors)
    wide_both = widen(jnp.concatenate([raw, vectors], axis=0))
    wide_raw, wide_vectors = wide_both[:16], wide_both[16:]

    def step_tables(raw_rows, vector_rows, strand, param):
        rows8 = letter_rows(raw_rows, letters, 8, complement if strand else None)
        shifted = rows8 + vector_rows[param : param + 1]
        step = jnp.maximum(shifted, 0.0) + jnp.log1p(jnp.exp(-jnp.abs(shifted)))
        decay = -vector_rows[2 + param : 3 + param] * step * LOG2E
        return step, decay, jnp.log2(step)

    lane8 = iota((8, LANES), 1)
    exponents = [jnp.zeros((8, LANES), F32)] * 3
    talls = []
    for index4, (falls, strand, param) in enumerate(PASSES):
        _, decay, log_step = step_tables(wide_raw, wide_vectors, strand, param)
        coefs_ref[index4, 0:8] = decay
        coefs_ref[index4, 8:16] = log_step
        coefs_ref[index4, 16:24] = jnp.broadcast_to(wide_vectors[4 + param : 5 + param], (8, inner))
        step, decay, log_step = step_tables(raw, vectors, strand, param)
        for place, narrow in enumerate((decay, log_step, step)):
            wide = jnp.concatenate([narrow, jnp.zeros((8, LANES - heads), F32)], axis=1)
            wide = pltpu.roll(wide, index4 * heads, 1) if index4 else wide
            mine = (lane8 >= index4 * heads) & (lane8 < (index4 + 1) * heads)
            exponents[place] = jnp.where(mine, wide, exponents[place])
    only = iota((8, LANES), 0) < letters
    tall = jnp.concatenate([exponents[0], jnp.zeros((LANES - 8, LANES), F32)], axis=0).T
    exponents = [
        jnp.concatenate([jnp.where(only, x, 0.0), jnp.zeros((8, LANES), F32)], axis=0)
        for x in exponents
    ]
    for place in range(2):
        rest = jnp.zeros((LANES - 48, LANES), BF16)
        exponent_ref[place] = jnp.concatenate([*split3(exponents[place]), rest], axis=0)
    word_steps = dot(last_ref[...], pack_split(exponents[2], 2))

    talls = [
        [
            jnp.broadcast_to(tall[k * 2 * heads : (k + 1) * 2 * heads, l : l + 1], (2 * heads, BLOCK))
            for l in range(letters)
        ]
        for k in range(2)
    ]
    for block in range(blocks):
        rises, falls = block < first, block >= past
        power = sum(
            counts[l][block : block + 1] * jnp.where(rises, talls[0][l], talls[1][l])
            for l in range(letters)
        )
        weight = jnp.exp2(power)
        lanes = slice(block * BLOCK, (block + 1) * BLOCK)
        weight_ref[: 2 * heads, lanes] = jnp.where(rises, weight, 0.0).astype(BF16)
        weight_ref[2 * heads :, lanes] = jnp.where(falls, weight, 0.0).astype(BF16)
    word_weights = dot(match_ref[...], weight_ref[...], NT)
    word_weights = (word_weights * word_steps[:, : 4 * heads]).astype(BF16)

    narrows = []
    for matches, hot, hot16, tallies, between, totals, doubled in prepared:
        up, down = tallies[:BLOCK], tallies[BLOCK:]
        powers = dot(
            jnp.concatenate([up, down, down - hot, up - hot], axis=0).astype(BF16), exponent_ref[0]
        )
        power = lambda k: powers[k * BLOCK : (k + 1) * BLOCK]
        rising = lane < 2 * heads
        from_start = jnp.exp2(jnp.where(rising, power(0), power(1)))
        steps = dot(hot16, exponent_ref[1])
        to_end = jnp.exp2(jnp.where(rising, power(2), power(3)) + steps)
        narrows.append(
            jnp.concatenate([from_start, to_end], axis=0).astype(BF16)[:, : 4 * heads]
        )

    for copy in reads[8:]:
        copy.wait()
    projected = dot(embedding, in_weight_ref[...]).astype(BF16).astype(F32)
    gate = silu(projected[:, :inner])
    for strand in range(2):
        gate_rows = letter_rows(gate, letters, 16, complement if strand else None)
        gate_rows = jnp.where(iota((16, 1), 0) < letters, gate_rows, 0.0)
        gates_ref[strand] = pack_split(gate_rows, 2)

    block_chunk = t // CHUNK
    lane_chunk = u // CHUNK
    head_of = iota((CHUNK, WIDE), 1) // head
    head_masks = [as_bf16(head_of == h) for h in range(WIDE // head)]
    scales = []
    for index4, (falls, strand, param) in enumerate(PASSES):
        d = int(falls)
        inputs = letter_rows(
            projected[:, inner:], letters, part_rows, complement if strand else None
        )
        tap_row = iota((part_rows, 1), 0) // letters
        weights = jnp.zeros((part_rows, inputs.shape[1]), F32)
        for tap in range(taps):
            weights = jnp.where(tap_row == tap, conv_weight_ref[param, tap : tap + 1, :], weights)
        bias_rows = jnp.zeros((part_rows, inputs.shape[1]), F32)
        for place, piece in enumerate(split3(conv_bias_ref[param : param + 1, :])):
            bias_rows = jnp.where(iota((part_rows, 1), 0) == place, piece.astype(F32), bias_rows)
        products = jnp.concatenate([*split3(weights * inputs), bias_rows.astype(BF16)], axis=0)
        conved = silu(dot(select_ref[...], products))
        words_ref[:, :inner] = conved[:, :inner].astype(BF16)
        rest = conved[:, inner:]
        rest_lane = iota(rest.shape, 1)
        words_ref[:, inner : inner + LANES] = jnp.where(
            rest_lane < state, pltpu.roll(rest, LANES - state, 1), 0.0
        ).astype(BF16)
        turned = rest.T[:state].astype(BF16)
        to_lanes = spread_rows(spread, index4, 4)
        weighted = (dot(word_weights, to_lanes) * conved[:, :inner]).astype(BF16)
        held = dot(turned, weighted)

        decay = [coefs_ref[index4, l : l + 1] for l in range(letters)]
        log_step = [coefs_ref[index4, 8 + l : 9 + l] for l in range(letters)]
        skip = coefs_ref[index4, 16:17]
        squares = []
        for part in range(own - 1, -1, -1) if falls else range(own):
            matches, _, hot16, _, between, totals, doubled = prepared[part]
            match, at = matches[d], part * BLOCK
            order = range(chunks - 1, -1, -1) if falls else range(chunks)
            bt = dot(turned, match, NT)
            c_rows = dot(match, words_ref[:, inner : inner + LANES])
            values = dot(match, words_ref[:, :inner])
            spreads = dot(narrows[part], to_lanes)
            all_scores = dot(c_rows.astype(BF16)[:, :state], bt.astype(BF16))
            bt_lane = iota(bt.shape, 1) // CHUNK
            bt_chunks = jnp.concatenate(
                [jnp.where(bt_lane == i, bt, 0.0).astype(BF16) for i in range(chunks)], axis=0
            )
            fresh = dot(bt_chunks, (values * spreads[BLOCK:]).astype(BF16))
            values16 = values.astype(BF16)
            scores = []
            for i in range(chunks):
                lanes = slice((i // 2) * LANES, (i // 2 + 1) * LANES)
                window = all_scores[i * CHUNK : (i + 1) * CHUNK, lanes]
                keep = (small_lane // CHUNK) == i % 2
                both = jnp.where(keep, window, pltpu.roll(window, CHUNK, 1))
                causal = (small_half >= small_row) if falls else (small_half <= small_row)
                scores.append(jnp.where(causal, both, 0.0))
            entering = [None] * chunks
            for i in order:
                entering[i] = held.astype(BF16)
                power_sum = jnp.zeros((1, inner), F32)
                for l in range(letters):
                    row = totals[i * letters + l : i * letters + l + 1]
                    row = jnp.concatenate([row] * (inner // LANES), axis=1)
                    power_sum = power_sum + row * decay[l]
                held = fresh[i * state : (i + 1) * state] + held * jnp.exp2(power_sum)
            twice = c_rows + pltpu.roll(c_rows, state, 1)
            c_chunks = jnp.concatenate([twice] * (chunks * state // LANES), axis=1)
            c_chunks = jnp.where(block_chunk == lane_chunk, c_chunks, 0.0).astype(BF16)
            carried = dot(c_chunks, jnp.concatenate(entering, axis=0))
            base_ref[...] = carried * spreads[:BLOCK] + skip * values
            square = [None] * chunks
            for group in range(inner // WIDE):
                wide = slice(group * WIDE, (group + 1) * WIDE)
                mixed, stacked = [], []
                for i in range(chunks):
                    mixing = []
                    for tile in range(WIDE // LANES):
                        low = group * WIDE + tile * LANES
                        lanes = slice(low, low + LANES)
                        total = log_step[0][:, lanes]
                        for l in range(1, letters):
                            total = jnp.where(doubled[i] == l, log_step[l][:, lanes], total)
                        for l in range(letters):
                            apart = between[d][l * BLOCK + i * CHUNK : l * BLOCK + (i + 1) * CHUNK]
                            total = total + apart * decay[l][:, lanes]
                        mixing.append((jnp.exp2(total) * scores[i]).astype(BF16))
                    mixed.append(jnp.concatenate(mixing, axis=1))
                    chunk_values = values16[i * CHUNK : (i + 1) * CHUNK, wide]
                    stacked.append(
                        jnp.concatenate([chunk_values * mask for mask in head_masks], axis=0)
                    )
                inside = [dot(m, v) for m, v in zip(mixed, stacked)]
                gate = dot(hot16[:, :32], gates_ref[strand, :, wide])
                for i in range(chunks):
                    chunk = slice(i * CHUNK, (i + 1) * CHUNK)
                    gated = (inside[i] + base_ref[chunk, wide]) * gate[chunk]
                    gated_ref[index4, at + i * CHUNK : at + (i + 1) * CHUNK, wide] = gated
                    part_sum = jnp.sum(gated * gated, axis=1, keepdims=True)
                    square[i] = part_sum if square[i] is None else square[i] + part_sum
            squares.append(jnp.concatenate(square, axis=0))
        squares = squares[::-1] if falls else squares
        scales.append(lax.rsqrt(jnp.concatenate(squares, axis=0) * (1.0 / inner) + EPSILON))
    for group in range(inner // WIDE):
        wide = slice(group * WIDE, (group + 1) * WIDE)
        total = None
        for index4, (falls, strand, param) in enumerate(PASSES):
            normed = gated_ref[index4, :, wide] * scales[index4] * gain_ref[param : param + 1, wide]
            total = normed if total is None else total + normed
        mixed_ref[:, wide] = total.astype(BF16)
    copy = pltpu.make_async_copy(mixed_ref, mixed_hbm, out_sem)
    copy.start()
    copy.wait()


def output_kernel(depth, places, here_ref, mixed_hbm, *refs):
    pieces = refs[: len(places)]
    out_ref, weight_ref, mixed_ref, sem = refs[len(places) :]
    here = here_ref[0]
    pairs = [(mixed_hbm, mixed_ref)]
    for piece, masks in zip(pieces, places):
        for k, mask in enumerate(masks):
            row = pl.multiple_of((here ^ mask) * depth, depth)
            pairs.append((piece.at[k], weight_ref.at[pl.ds(row, depth)]))
    for copy in start_all(pairs, sem):
        copy.wait()
    out_ref[...] = dot(mixed_ref[...], weight_ref[...]).astype(BF16)


def swap(x, axis, mask):
    count = lax.axis_size(axis)
    return lax.ppermute(x, axis, [(i, i ^ mask) for i in range(count)])


def vmem():
    return pl.BlockSpec(memory_space=pltpu.VMEM)


def hbm():
    return pl.BlockSpec(memory_space=pltpu.HBM)


def smem():
    return pl.BlockSpec(memory_space=pltpu.SMEM)


def on_device(
    token_ids,
    complement,
    embedding,
    in_weight,
    step_weight,
    conv_weight,
    conv_bias,
    step_bias,
    decay_rate,
    skip_gain,
    norm_gain,
    out_weight,
):
    genomes, rows = token_ids.shape
    letters, width = embedding.shape
    taps = conv_weight.shape[1]
    heads = step_weight.shape[1]
    inner = norm_gain.shape[1]
    state = (conv_weight.shape[2] - inner) // 2
    count, sides = lax.axis_size("seq"), lax.axis_size("batch")
    here = lax.axis_index("seq").astype(jnp.int32)[None]
    side = lax.axis_index("batch").astype(jnp.int32)[None]
    depth, columns = out_weight.shape

    bits = [1 << k for k in range(count.bit_length() - 1)]
    join = lambda *x: jnp.concatenate(x, axis=0)
    moved = lambda masks, mask: [m ^ mask for m in masks]
    tokens, token_bits = token_ids[None], list(bits)
    line, line_masks = out_weight[None], [0]
    for mask in bits[:1:-1]:
        arrived = swap(line, "seq", mask)
        if token_bits:
            tokens = join(tokens, swap(tokens, "seq", token_bits.pop(0)))
        line = join(line, arrived)
        line_masks = line_masks + moved(line_masks, mask)
        line, tokens = lax.optimization_barrier((line, tokens))
    while token_bits:
        tokens = join(tokens, swap(tokens, "seq", token_bits.pop(0)))
    across_plane = [swap(line, "seq", mask) for mask in (1, 2, 3)]
    places = [line_masks] + [moved(line_masks, mask) for mask in (1, 2, 3)]

    select, last = word_select(letters, taps)
    word_rows = select.shape[0]
    spread = np.repeat(np.eye(heads, dtype=np.float32), inner // heads, axis=1).astype(
        ml_dtypes.bfloat16
    )
    mixed = []
    for genome in range(genomes):
        inputs = (
            tokens[:, genome],
            spread,
            embedding,
            step_weight.T,
            step_bias,
            decay_rate,
            skip_gain,
            last,
            select,
            conv_weight,
            conv_bias,
            norm_gain,
            in_weight,
        )
        mixed.append(
            pl.pallas_call(
                partial(mixer_kernel, letters, taps, state, count),
                out_shape=jax.ShapeDtypeStruct((rows, inner), BF16),
                in_specs=[smem(), smem()] + [hbm()] * len(inputs),
                out_specs=hbm(),
                scratch_shapes=[pltpu.VMEM(x.shape, x.dtype) for x in inputs]
                + [
                    pltpu.VMEM((rows, inner), BF16),
                    pltpu.VMEM((word_rows, inner + LANES), BF16),
                    pltpu.VMEM((2, 32, inner), BF16),
                    pltpu.VMEM((4, 24, inner), F32),
                    pltpu.VMEM((2, LANES, LANES), BF16),
                    pltpu.VMEM((word_rows, count * rows), BF16),
                    pltpu.VMEM((4 * heads, count * rows), BF16),
                    pltpu.VMEM((BLOCK, inner), F32),
                    pltpu.VMEM((4, rows, inner), F32),
                    pltpu.SemaphoreType.DMA((len(inputs),)),
                    pltpu.SemaphoreType.DMA,
                ],
                compiler_params=pltpu.CompilerParams(vmem_limit_bytes=VMEM_BYTES),
                cost_estimate=pl.CostEstimate(
                    flops=10**10, bytes_accessed=50 * 2**20, transcendentals=2**22
                ),
                name="mixer",
            )(here, complement, *inputs)
        )
    line, across_plane, mixed = lax.optimization_barrier((line, across_plane, mixed))
    pieces = [line, *across_plane]
    sets = [(pieces, 0)]
    mask = 1
    while mask < sides:
        sets = sets + [([swap(x, "batch", mask) for x in found], s ^ mask) for found, s in sets]
        mask *= 2

    def project(found, mixed):
        return pl.pallas_call(
            partial(output_kernel, depth, places),
            out_shape=jax.ShapeDtypeStruct((rows, columns), BF16),
            in_specs=[smem()] + [hbm()] * (1 + len(found)),
            out_specs=vmem(),
            scratch_shapes=[
                pltpu.VMEM((depth * count, columns), BF16),
                pltpu.VMEM((rows, inner), BF16),
                pltpu.SemaphoreType.DMA((count + 1,)),
            ],
            compiler_params=pltpu.CompilerParams(vmem_limit_bytes=16 * 2**20),
            cost_estimate=pl.CostEstimate(
                flops=2 * rows * inner * columns, bytes_accessed=2**22, transcendentals=0
            ),
            name="output",
        )(here, mixed, *found)

    results = []
    for genome in range(genomes):
        parts = [project(found, mixed[genome]) for found, _ in sets]
        ordered = []
        for k in range(sides):
            chosen = parts[0]
            for part, (_, part_side) in zip(parts, sets):
                chosen = jnp.where((side[0] ^ part_side) == k, part, chosen)
            ordered.append(chosen)
        results.append(jnp.concatenate(ordered, axis=1))
    return jnp.stack(results)


def solution(mesh):
    placed = (P("batch", "seq"),) + (P(),) * 10 + (P("seq", "batch"),)
    return jax.shard_map(
        on_device, mesh=mesh, in_specs=placed, out_specs=P("batch", "seq", None), check_vma=False
    )
```

```python
from functools import partial

import jax
import jax.numpy as jnp
import ml_dtypes
import numpy as np
from jax import lax
from jax.experimental import pallas as pl
from jax.experimental.pallas import tpu as pltpu
from jax.sharding import PartitionSpec as P

BLOCK = 256
CHUNK = 64
LANES = 128
WIDE = 256
LOG2E = 1.4426950408889634
EPSILON = 1e-05
VMEM_BYTES = 64 * 2**20
F32 = jnp.float32
BF16 = jnp.bfloat16

TN = (((0,), (0,)), ((), ()))
NT = (((1,), (1,)), ((), ()))
NN = (((1,), (0,)), ((), ()))


def dot(a, b, dims=NN):
    return lax.dot_general(a, b, dims, preferred_element_type=F32)


def iota(shape, dim):
    return lax.broadcasted_iota(jnp.int32, shape, dim)


def split3(x):
    high = x.astype(BF16)
    rest = x - high.astype(F32)
    middle = rest.astype(BF16)
    low = (rest - middle.astype(F32)).astype(BF16)
    return high, middle, low


def silu(x):
    return x / (1.0 + jnp.exp(-x))


def word_select(letters, taps):
    part = -(-letters * taps // 16) * 16
    codes = np.arange(letters**taps)
    select = np.zeros((len(codes), 4 * part), np.float32)
    last = np.zeros((len(codes), 32), np.float32)
    for back in range(taps):
        letter = codes // letters**back % letters
        for copy in range(3):
            select[codes, copy * part + (taps - 1 - back) * letters + letter] = 1
    select[:, 3 * part : 3 * part + 3] = 1
    for copy in range(2):
        last[codes, copy * 16 + codes % letters] = 1
    return select.astype(ml_dtypes.bfloat16), last.astype(ml_dtypes.bfloat16)


PASSES = ((False, 0, 0), (False, 1, 1), (True, 0, 1), (True, 1, 0))


def letter_rows(table, letters, rows, complement):
    row = iota((rows, 1), 0) % letters
    picked = row
    if complement is not None:
        picked = jnp.zeros_like(row)
        for letter in range(letters):
            picked = jnp.where(row == letter, complement(letter), picked)
    result = jnp.broadcast_to(table[0:1], (rows, table.shape[1]))
    for letter in range(1, letters):
        result = jnp.where(picked == letter, table[letter : letter + 1], result)
    return result


def pack_split(x, copies):
    return jnp.concatenate(split3(x)[:copies], axis=0)


def start_all(pairs, sems):
    copies = [
        pltpu.make_async_copy(source, target, sems.at[k]) for k, (source, target) in enumerate(pairs)
    ]
    for copy in copies:
        copy.start()
    return copies


def word_index(both, start, size, falls, taps, letters, before_end):
    lanes = both.shape[1]
    codes, scale = None, 1
    for back in range(taps):
        turned = both if back == 0 else pltpu.roll(both, lanes - back if falls else back, 1)
        part = scale * turned[:, start : start + size]
        codes = part if codes is None else codes + part
        scale *= letters
    return jnp.where(before_end < taps - 1, scale + before_end, codes)


def first_words(tokens, letters, taps, part, width):
    row, col = iota((16, width), 0), iota((16, width), 1)
    inner_col = col % part
    found = (col >= 3 * part) & (col < 3 * part + 3)
    for length in range(1, taps):
        for back in range(length):
            want = (taps - 1 - back) * letters + tokens[length - 1 - back]
            found = found | ((row == length - 1) & (col < 3 * part) & (inner_col == want))
    return jnp.where(found & (row < taps - 1), 1.0, 0.0).astype(BF16)


def first_last(tokens, letters, taps):
    row, col = iota((16, 32), 0), iota((16, 32), 1) % 16
    found = jnp.zeros((16, 32), jnp.bool_)
    for length in range(1, taps):
        found = found | ((row == length - 1) & (col == tokens[length - 1]))
    return jnp.where(found, 1.0, 0.0).astype(BF16)


def spread_rows(spread, index, count):
    heads = spread.shape[0]
    stacked = jnp.concatenate([spread] * count, axis=0)
    return jnp.where(iota(stacked.shape, 0) // heads == index, stacked, jnp.zeros_like(stacked))


def mixer_kernel(
    letters,
    taps,
    state,
    count,
    here_ref,
    complement_ref,
    *refs,
):
    token_hbms, refs = refs[:4], refs[4:]
    (
        spread_hbm,
        embedding_hbm,
        step_weight_hbm,
        step_bias_hbm,
        rate_hbm,
        skip_hbm,
        last_hbm,
        select_hbm,
        conv_weight_hbm,
        conv_bias_hbm,
        gain_hbm,
        in_weight_hbm,
        mixed_hbm,
        tokens_ref,
        spread_ref,
        embedding_ref,
        step_weight_ref,
        step_bias_ref,
        rate_ref,
        skip_ref,
        last_ref,
        select_ref,
        conv_weight_ref,
        conv_bias_ref,
        gain_ref,
        in_weight_ref,
        mixed_ref,
        words_ref,
        gates_ref,
        coefs_ref,
        exponent_ref,
        match_ref,
        weight_ref,
        base_ref,
        gated_ref,
        gate_ref,
        in_sems,
        out_sem,
    ) = refs
    reads = start_all(
        (
            *((hbm, tokens_ref.at[k]) for k, hbm in enumerate(token_hbms)),
            (spread_hbm, spread_ref),
            (embedding_hbm, embedding_ref),
            (step_weight_hbm, step_weight_ref),
            (step_bias_hbm, step_bias_ref),
            (rate_hbm, rate_ref),
            (skip_hbm, skip_ref),
            (last_hbm, last_ref),
            (select_hbm, select_ref),
            (conv_weight_hbm, conv_weight_ref),
            (conv_bias_hbm, conv_bias_ref),
            (gain_hbm, gain_ref),
            (in_weight_hbm, in_weight_ref),
        ),
        in_sems,
    )
    here = here_ref[0]
    rows = tokens_ref.shape[2]
    own = rows // BLOCK
    blocks = count * own
    heads, inner = spread_ref.shape
    head = inner // heads
    full = select_ref.shape[0]
    part_rows = select_ref.shape[1] // 4
    first, past = here * own, (here + 1) * own
    chunks = BLOCK // CHUNK
    as_bf16 = lambda mask: jnp.where(mask, 1.0, 0.0).astype(BF16)
    complement = lambda letter: complement_ref[letter]

    for copy in reads[:4]:
        copy.wait()
    tokens16 = jnp.concatenate([tokens_ref[k] for k in range(4)], axis=0).astype(F32).astype(BF16)
    place, target = iota((blocks, count), 1), iota((blocks, count), 0)
    source = here ^ (place % (count // 4) * 4 + place // (count // 4))
    around = jnp.zeros((3 * blocks, BLOCK), F32)
    for part in range(own):
        block = source * own + part
        pick = jnp.concatenate([as_bf16(block == target + k) for k in (-1, 0, 1)], axis=0)
        around = around + dot(pick, tokens16[:, part * BLOCK : (part + 1) * BLOCK])
    around = around.astype(jnp.int32)
    before, middle, after = (around[k * blocks : (k + 1) * blocks] for k in range(3))
    position = iota((blocks, BLOCK), 0) * BLOCK + iota((blocks, BLOCK), 1)
    rise_index = word_index(
        jnp.concatenate([before, middle], axis=1), BLOCK, BLOCK, False, taps, letters, position
    )
    fall_index = word_index(
        jnp.concatenate([middle, after], axis=1),
        0,
        BLOCK,
        True,
        taps,
        letters,
        blocks * BLOCK - 1 - position,
    )
    block_of = iota((blocks, BLOCK), 0)
    middle_word = full // 2
    word = (iota((full + 16, BLOCK), 0) - middle_word).astype(F32).astype(BF16)
    index = jnp.where(block_of < first, rise_index, fall_index) - middle_word
    index = index.astype(F32).astype(BF16)
    one, zero = jnp.ones((), BF16), jnp.zeros((), BF16)
    for block in range(blocks):
        match_ref[:, block * BLOCK : (block + 1) * BLOCK] = jnp.where(
            word[:full] == index[block : block + 1], one, zero
        )
    ends = [
        jnp.where(word[full:] == index[block : block + 1], one, zero) for block in (0, blocks - 1)
    ]

    end_tokens = (
        [middle[:1, k : k + 1] for k in range(taps - 1)],
        [middle[blocks - 1 :, BLOCK - 1 - k : BLOCK - k] for k in range(taps - 1)],
    )

    letter_hot = [jnp.where(middle == letter, 1.0, 0.0) for letter in range(letters)]
    stack = jnp.concatenate(letter_hot, axis=0).astype(BF16)
    t = iota((BLOCK, BLOCK), 0)
    u = iota((BLOCK, BLOCK), 1)
    sums = dot(stack, jnp.concatenate([as_bf16(t <= u), jnp.ones((BLOCK, BLOCK), BF16)], axis=1))
    running, block_sum = sums[:, :BLOCK], sums[:, BLOCK:].astype(BF16)
    col, row = iota((blocks, blocks), 1), iota((blocks, blocks), 0)
    to_rise = as_bf16((col >= row) & (col < first))
    to_fall = as_bf16((col >= past) & (col < row))
    both_ways = jnp.concatenate([to_rise, to_fall], axis=0)
    counts = []
    for letter in range(letters):
        part = slice(letter * blocks, (letter + 1) * blocks)
        far = dot(both_ways, block_sum[part])
        rise = far[:blocks] - running[part]
        fall = far[blocks:] + running[part] - letter_hot[letter]
        counts.append(jnp.where(block_of < first, rise, fall))

    same = (t // CHUNK) == (u // CHUNK)
    until, since = as_bf16(same & (u <= t)), as_bf16(same & (u >= t))
    half = iota((BLOCK, LANES), 1) % CHUNK
    inside_row = iota((BLOCK, LANES), 0) % CHUNK
    lane = iota((BLOCK, LANES), 1)
    hot_lane = jnp.where(lane < 48, (lane % 16).astype(F32), -1.0)
    word_lane = iota((BLOCK, full), 1).astype(F32)
    end_lane = (iota((16, 16), 1) + full).astype(F32)
    small_half = iota((CHUNK, LANES), 1) % CHUNK
    small_row = iota((CHUNK, LANES), 0)
    small_lane = iota((CHUNK, LANES), 1)
    row_lane = iota((1, LANES), 1)
    beyond = (as_bf16(inside_row > half), as_bf16(inside_row < half))
    row8 = iota((8, BLOCK), 0)
    prepared = []
    for part in range(own):
        mine = block_of == first + part
        take = lambda x: jnp.sum(jnp.where(mine, x, 0), axis=0, keepdims=True)
        token_row = take(middle).astype(F32)
        facts = jnp.where(row8 == 0, take(rise_index), take(fall_index)).astype(F32)
        facts = jnp.where(row8 == 2, token_row, facts)
        facts = jnp.concatenate([facts, jnp.zeros((LANES - 8, BLOCK), F32)], axis=0).T
        matches = [
            jnp.where(word_lane == facts[:, d : d + 1], 1.0, 0.0).astype(BF16) for d in range(2)
        ]
        matches += [
            jnp.where(end_lane == facts[at : at + 16, d : d + 1], 1.0, 0.0).astype(BF16)
            for d, at in ((0, 0), (1, BLOCK - 16))
        ]
        hot = jnp.where(hot_lane == facts[:, 2:3], 1.0, 0.0)
        hot16 = hot.astype(BF16)
        tallies = dot(jnp.concatenate([until, since], axis=0), hot16)
        hot_rows = [jnp.where(token_row == l, 1.0, 0.0) for l in range(letters)]
        between = []
        for d, reach in enumerate((until, since)):
            left = jnp.concatenate([reach * h.astype(BF16) for h in hot_rows], axis=0)
            between.append(dot(left, beyond[d]))
        totals = jnp.concatenate(
            [jnp.where(u[:1] // CHUNK == i, h, 0.0) for i in range(chunks) for h in hot_rows],
            axis=0,
        ).astype(BF16)
        totals = dot(totals, jnp.ones((BLOCK, LANES), BF16))
        doubled = []
        for i in range(chunks):
            window = token_row[:, (i // 2) * LANES : (i // 2 + 1) * LANES]
            keep = (row_lane // CHUNK) == i % 2
            doubled.append(jnp.where(keep, window, pltpu.roll(window, CHUNK, 1)))
        prepared.append((matches, hot, hot16, tallies, between, totals, doubled))

    for copy in reads[4:11]:
        copy.wait()
    spread = spread_ref[...]
    width = embedding_ref.shape[1]
    embedding = jnp.concatenate(
        [embedding_ref[...], jnp.zeros((16 - letters, width), BF16)], axis=0
    )
    raw = dot(embedding, step_weight_ref[...], NT)

    def widen(x):
        return sum(dot(piece, spread) for piece in split3(x))

    row = iota((16, heads), 0)
    vectors = jnp.zeros((16, heads), F32)
    for k in range(2):
        vectors = jnp.where(row == k, step_bias_ref[k : k + 1, :], vectors)
        vectors = jnp.where(row == 2 + k, rate_ref[k : k + 1, :], vectors)
        vectors = jnp.where(row == 4 + k, skip_ref[k : k + 1, :], vectors)
    wide_both = widen(jnp.concatenate([raw, vectors], axis=0))
    wide_raw, wide_vectors = wide_both[:16], wide_both[16:]

    def step_tables(raw_rows, vector_rows, strand, param):
        rows8 = letter_rows(raw_rows, letters, 8, complement if strand else None)
        shifted = rows8 + vector_rows[param : param + 1]
        step = jnp.maximum(shifted, 0.0) + jnp.log1p(jnp.exp(-jnp.abs(shifted)))
        decay = -vector_rows[2 + param : 3 + param] * step * LOG2E
        return step, decay, jnp.log2(step)

    lane8 = iota((8, LANES), 1)
    exponents = [jnp.zeros((8, LANES), F32)] * 3
    talls = []
    for index4, (falls, strand, param) in enumerate(PASSES):
        _, decay, log_step = step_tables(wide_raw, wide_vectors, strand, param)
        coefs_ref[index4, 0:8] = decay
        coefs_ref[index4, 8:16] = log_step
        coefs_ref[index4, 16:24] = jnp.broadcast_to(wide_vectors[4 + param : 5 + param], (8, inner))
        step, decay, log_step = step_tables(raw, vectors, strand, param)
        for place, narrow in enumerate((decay, log_step, step)):
            wide = jnp.concatenate([narrow, jnp.zeros((8, LANES - heads), F32)], axis=1)
            wide = pltpu.roll(wide, index4 * heads, 1) if index4 else wide
            mine = (lane8 >= index4 * heads) & (lane8 < (index4 + 1) * heads)
            exponents[place] = jnp.where(mine, wide, exponents[place])
    only = iota((8, LANES), 0) < letters
    tall = jnp.concatenate([exponents[0], jnp.zeros((LANES - 8, LANES), F32)], axis=0).T
    exponents = [
        jnp.concatenate([jnp.where(only, x, 0.0), jnp.zeros((8, LANES), F32)], axis=0)
        for x in exponents
    ]
    for place in range(2):
        rest = jnp.zeros((LANES - 48, LANES), BF16)
        exponent_ref[place] = jnp.concatenate([*split3(exponents[place]), rest], axis=0)
    lasts = [last_ref[...]] + [first_last(x, letters, taps) for x in end_tokens]
    word_steps = dot(jnp.concatenate(lasts, axis=0), pack_split(exponents[2], 2))

    talls = [
        [
            jnp.broadcast_to(tall[k * 2 * heads : (k + 1) * 2 * heads, l : l + 1], (2 * heads, BLOCK))
            for l in range(letters)
        ]
        for k in range(2)
    ]
    for block in range(blocks):
        rises, falls = block < first, block >= past
        power = sum(
            counts[l][block : block + 1] * jnp.where(rises, talls[0][l], talls[1][l])
            for l in range(letters)
        )
        weight = jnp.exp2(power)
        lanes = slice(block * BLOCK, (block + 1) * BLOCK)
        weight_ref[: 2 * heads, lanes] = jnp.where(rises, weight, 0.0).astype(BF16)
        weight_ref[2 * heads :, lanes] = jnp.where(falls, weight, 0.0).astype(BF16)
    word_weights = dot(match_ref[...], weight_ref[...], NT)
    end_weights = [
        dot(end, weight_ref[:, block * BLOCK : (block + 1) * BLOCK], NT)
        for end, block in zip(ends, (0, blocks - 1))
    ]
    word_weights = jnp.concatenate([word_weights, *end_weights], axis=0)
    word_weights = (word_weights * word_steps[:, : 4 * heads]).astype(BF16)
    end_selects = [
        first_words(x, letters, taps, part_rows, 4 * part_rows) for x in end_tokens
    ]

    narrows = []
    for matches, hot, hot16, tallies, between, totals, doubled in prepared:
        up, down = tallies[:BLOCK], tallies[BLOCK:]
        powers = dot(
            jnp.concatenate([up, down, down - hot, up - hot], axis=0).astype(BF16), exponent_ref[0]
        )
        power = lambda k: powers[k * BLOCK : (k + 1) * BLOCK]
        steps = dot(hot16, exponent_ref[1])
        chunk_power = [power(0)[(i + 1) * CHUNK - 1 : (i + 1) * CHUNK] for i in range(chunks)]
        found = []
        for falls in (False, True):
            ends_at = power(2 + falls) + steps
            pieces = [power(int(falls))]
            for i in range(chunks + 1):
                target = chunks - 1 - i if falls else i
                if i == chunks and own == 1:
                    continue
                for j in range(chunks):
                    passed = range(target + 1, j) if falls else range(j + 1, target)
                    if (j > target) if falls else (j < target):
                        pieces.append(
                            ends_at[j * CHUNK : (j + 1) * CHUNK] + sum(chunk_power[m] for m in passed)
                        )
            found.append(jnp.exp2(jnp.concatenate(pieces, axis=0)).astype(BF16)[:, : 4 * heads])
        narrows.append(found)

    for copy in reads[11:]:
        copy.wait()
    projected = dot(embedding, in_weight_ref[...]).astype(BF16).astype(F32)
    gate = silu(projected[:, :inner])
    for strand in range(2):
        gate_rows = letter_rows(gate, letters, 16, complement if strand else None)
        gate_rows = jnp.where(iota((16, 1), 0) < letters, gate_rows, 0.0)
        gates_ref[strand] = pack_split(gate_rows, 2)

    block_chunk = t // CHUNK
    lane_chunk = u // CHUNK
    head_of = iota((CHUNK, WIDE), 1) // head
    head_masks = [as_bf16(head_of == h) for h in range(WIDE // head)]
    scales = []
    for index4, (falls, strand, param) in enumerate(PASSES):
        d = int(falls)
        inputs = letter_rows(
            projected[:, inner:], letters, part_rows, complement if strand else None
        )
        tap_row = iota((part_rows, 1), 0) // letters
        weights = jnp.zeros((part_rows, inputs.shape[1]), F32)
        for tap in range(taps):
            weights = jnp.where(tap_row == tap, conv_weight_ref[param, tap : tap + 1, :], weights)
        bias_rows = jnp.zeros((part_rows, inputs.shape[1]), F32)
        for place, piece in enumerate(split3(conv_bias_ref[param : param + 1, :])):
            bias_rows = jnp.where(iota((part_rows, 1), 0) == place, piece.astype(F32), bias_rows)
        products = jnp.concatenate([*split3(weights * inputs), bias_rows.astype(BF16)], axis=0)
        select = jnp.concatenate([select_ref[...], end_selects[d]], axis=0)
        conved = silu(dot(select, products))
        words_ref[:, :inner] = conved[:, :inner].astype(BF16)
        rest = conved[:, inner:]
        rest_lane = iota(rest.shape, 1)
        words_ref[:, inner : inner + LANES] = jnp.where(
            rest_lane < state, pltpu.roll(rest, LANES - state, 1), 0.0
        ).astype(BF16)
        turned = rest.T[:state].astype(BF16)
        to_lanes = spread_rows(spread, index4, 4)
        own_weights = jnp.concatenate(
            [word_weights[:full], word_weights[full + 16 * d : full + 16 * (d + 1)]], axis=0
        )
        weighted = (dot(own_weights, to_lanes) * conved[:, :inner]).astype(BF16)
        held = dot(turned, weighted)

        decay = [coefs_ref[index4, l : l + 1] for l in range(letters)]
        log_step = [coefs_ref[index4, 8 + l : 9 + l] for l in range(letters)]
        skip = coefs_ref[index4, 16:17]
        squares = []
        for part in range(own - 1, -1, -1) if falls else range(own):
            matches, _, hot16, _, between, totals, doubled = prepared[part]
            match, end_match, at = matches[d], matches[2 + d], part * BLOCK

            def looked_up(columns):
                found = dot(match, words_ref[:full, columns])
                more = dot(end_match, words_ref[full:, columns])
                if falls:
                    return jnp.concatenate([found[: BLOCK - 16], found[BLOCK - 16 :] + more], axis=0)
                return jnp.concatenate([found[:16] + more, found[16:]], axis=0)

            order = range(chunks - 1, -1, -1) if falls else range(chunks)
            end_bt = dot(turned[:, full:], end_match, NT)
            bt = dot(turned[:, :full], match, NT)
            if falls:
                bt = jnp.concatenate([bt[:, : BLOCK - 16], bt[:, BLOCK - 16 :] + end_bt], axis=1)
            else:
                bt = jnp.concatenate([bt[:, :16] + end_bt, bt[:, 16:]], axis=1)
            c_rows = looked_up(slice(inner, inner + LANES))
            values = looked_up(slice(0, inner))
            spreads = dot(narrows[part][d], to_lanes)
            c16, bt16 = c_rows.astype(BF16)[:, :state], bt.astype(BF16)
            all_scores = dot(c16, bt16)
            values16 = values.astype(BF16)
            scores = []
            for i in range(chunks):
                lanes = slice((i // 2) * LANES, (i // 2 + 1) * LANES)
                window = all_scores[i * CHUNK : (i + 1) * CHUNK, lanes]
                keep = (small_lane // CHUNK) == i % 2
                both = jnp.where(keep, window, pltpu.roll(window, CHUNK, 1))
                causal = (small_half >= small_row) if falls else (small_half <= small_row)
                scores.append(jnp.where(causal, both, 0.0))
            twice = c_rows + pltpu.roll(c_rows, state, 1)
            c_chunks = jnp.concatenate([twice] * (chunks * state // LANES), axis=1)
            earlier = (lane_chunk > block_chunk) if falls else (lane_chunk < block_chunk)
            left = jnp.where(earlier, all_scores, 0.0)
            left = jnp.where(lane_chunk == block_chunk, c_chunks, left).astype(BF16)
            used = BLOCK
            power_sum = None
            pairs = LANES // CHUNK
            for i in order:
                decayed = held if power_sum is None else held * jnp.exp2(power_sum)
                blocks_of = [jnp.zeros((CHUNK, inner), BF16)] * chunks
                blocks_of[i] = decayed.astype(BF16)
                others = range(i + 1, chunks) if falls else range(i)
                for j in others:
                    rows_of = slice(j * CHUNK, (j + 1) * CHUNK)
                    blocks_of[j] = (values[rows_of] * spreads[used : used + CHUNK]).astype(BF16)
                    used += CHUNK
                low = (i // pairs) * pairs if falls else 0
                high = chunks if falls else (i // pairs + 1) * pairs
                chunk = slice(i * CHUNK, (i + 1) * CHUNK)
                carried = dot(
                    left[chunk, low * CHUNK : high * CHUNK],
                    jnp.concatenate(blocks_of[low:high], axis=0),
                )
                base_ref[chunk] = carried * spreads[chunk] + skip * values[chunk]
                for l in range(letters):
                    row = totals[i * letters + l : i * letters + l + 1]
                    row = jnp.concatenate([row] * (inner // LANES), axis=1) * decay[l]
                    power_sum = row if power_sum is None else power_sum + row
            if own > 1:
                fresh = dot(bt16, (values * spreads[used : used + BLOCK]).astype(BF16))
                held = held * jnp.exp2(power_sum) + fresh
            square = [None] * chunks
            for group in range(inner // WIDE):
                wide = slice(group * WIDE, (group + 1) * WIDE)
                mixed, stacked = [], []
                for i in range(chunks):
                    mixing = []
                    for tile in range(WIDE // LANES):
                        low = group * WIDE + tile * LANES
                        lanes = slice(low, low + LANES)
                        total = log_step[0][:, lanes]
                        for l in range(1, letters):
                            total = jnp.where(doubled[i] == l, log_step[l][:, lanes], total)
                        for l in range(letters):
                            apart = between[d][l * BLOCK + i * CHUNK : l * BLOCK + (i + 1) * CHUNK]
                            total = total + apart * decay[l][:, lanes]
                        mixing.append((jnp.exp2(total) * scores[i]).astype(BF16))
                    mixed.append(jnp.concatenate(mixing, axis=1))
                    chunk_values = values16[i * CHUNK : (i + 1) * CHUNK, wide]
                    stacked.append(
                        jnp.concatenate([chunk_values * mask for mask in head_masks], axis=0)
                    )
                inside = [dot(m, v) for m, v in zip(mixed, stacked)]
                if index4 == strand:
                    gate_ref[strand, at : at + BLOCK, wide] = dot(
                        hot16[:, :32], gates_ref[strand, :, wide]
                    )
                gate = gate_ref[strand, at : at + BLOCK, wide]
                for i in range(chunks):
                    chunk = slice(i * CHUNK, (i + 1) * CHUNK)
                    gated = (inside[i] + base_ref[chunk, wide]) * gate[chunk]
                    gated_ref[index4, at + i * CHUNK : at + (i + 1) * CHUNK, wide] = gated
                    part_sum = jnp.sum(gated * gated, axis=1, keepdims=True)
                    square[i] = part_sum if square[i] is None else square[i] + part_sum
            squares.append(jnp.concatenate(square, axis=0))
        squares = squares[::-1] if falls else squares
        scales.append(lax.rsqrt(jnp.concatenate(squares, axis=0) * (1.0 / inner) + EPSILON))
    for group in range(inner // WIDE):
        wide = slice(group * WIDE, (group + 1) * WIDE)
        total = 0.0
        for param in range(2):
            part = sum(
                gated_ref[k, :, wide] * scales[k] for k in range(len(PASSES)) if PASSES[k][2] == param
            )
            total = total + part * gain_ref[param : param + 1, wide]
        mixed_ref[:, wide] = total.astype(BF16)
    copy = pltpu.make_async_copy(mixed_ref, mixed_hbm, out_sem)
    copy.start()
    copy.wait()


def output_kernel(depth, places, flip, here_ref, side_ref, mixed_hbm, *refs):
    pieces = refs[: len(places)]
    out_hbm, weight_ref, mixed_ref, out_ref, sem, out_sem = refs[-6:]
    here, side = here_ref[0], side_ref[0]
    pairs = [(mixed_hbm, mixed_ref)]
    for piece, masks in zip(pieces, places):
        for k, mask in enumerate(masks):
            row = pl.multiple_of((here ^ mask) * depth, depth)
            pairs.append((piece.at[k], weight_ref.at[pl.ds(row, depth)]))
    for copy in start_all(pairs, sem):
        copy.wait()
    out_ref[...] = dot(mixed_ref[...], weight_ref[...]).astype(BF16)
    columns = out_ref.shape[1]
    lane = pl.multiple_of((side ^ flip) * columns, columns)
    copy = pltpu.make_async_copy(out_ref, out_hbm.at[:, pl.ds(lane, columns)], out_sem)
    copy.start()
    copy.wait()


def swap(x, axis, mask):
    count = lax.axis_size(axis)
    return lax.ppermute(x, axis, [(i, i ^ mask) for i in range(count)])


def vmem():
    return pl.BlockSpec(memory_space=pltpu.VMEM)


def hbm():
    return pl.BlockSpec(memory_space=pltpu.HBM)


def smem():
    return pl.BlockSpec(memory_space=pltpu.SMEM)


def on_device(
    token_ids,
    complement,
    embedding,
    in_weight,
    step_weight,
    conv_weight,
    conv_bias,
    step_bias,
    decay_rate,
    skip_gain,
    norm_gain,
    out_weight,
):
    genomes, rows = token_ids.shape
    letters, width = embedding.shape
    taps = conv_weight.shape[1]
    heads = step_weight.shape[1]
    inner = norm_gain.shape[1]
    state = (conv_weight.shape[2] - inner) // 2
    count, sides = lax.axis_size("seq"), lax.axis_size("batch")
    here = lax.axis_index("seq").astype(jnp.int32)[None]
    side = lax.axis_index("batch").astype(jnp.int32)[None]
    depth, columns = out_weight.shape

    join = lambda *x: jnp.concatenate(x, axis=0)
    moved = lambda masks, mask: [m ^ mask for m in masks]
    line, line_masks = out_weight[None], [0]
    tokens = token_ids[None]
    token_line = [swap(tokens, "seq", mask) for mask in range(count - 4, 0, -4)]
    mask = count // 2
    while mask > 2:
        arrived = swap(line, "seq", mask)
        if mask == count // 2:
            arrived, token_line = lax.optimization_barrier((arrived, token_line))
            token_line = join(tokens, *token_line[::-1])
            tokens = [token_line] + [swap(token_line, "seq", m) for m in (1, 2, 3)]
        line = join(line, arrived)
        line_masks = line_masks + moved(line_masks, mask)
        mask //= 2
    across_plane = [swap(line, "seq", mask) for mask in (1, 2, 3)]
    places = [line_masks] + [moved(line_masks, mask) for mask in (1, 2, 3)]

    select, last = word_select(letters, taps)
    word_rows = select.shape[0]
    spread = np.repeat(np.eye(heads, dtype=np.float32), inner // heads, axis=1).astype(
        ml_dtypes.bfloat16
    )
    mixed = []
    for genome in range(genomes):
        inputs = (
            *(x[:, genome] for x in tokens),
            spread,
            embedding,
            step_weight.T,
            step_bias,
            decay_rate,
            skip_gain,
            last,
            select,
            conv_weight,
            conv_bias,
            norm_gain,
            in_weight,
        )
        mixed.append(
            pl.pallas_call(
                partial(mixer_kernel, letters, taps, state, count),
                out_shape=jax.ShapeDtypeStruct((rows, inner), BF16),
                in_specs=[smem(), smem()] + [hbm()] * len(inputs),
                out_specs=hbm(),
                scratch_shapes=[pltpu.VMEM((4, *inputs[0].shape), jnp.int32)]
                + [pltpu.VMEM(x.shape, x.dtype) for x in inputs[4:]]
                + [
                    pltpu.VMEM((rows, inner), BF16),
                    pltpu.VMEM((word_rows + 16, inner + LANES), BF16),
                    pltpu.VMEM((2, 32, inner), BF16),
                    pltpu.VMEM((4, 24, inner), F32),
                    pltpu.VMEM((2, LANES, LANES), BF16),
                    pltpu.VMEM((letters**taps, count * rows), BF16),
                    pltpu.VMEM((4 * heads, count * rows), BF16),
                    pltpu.VMEM((BLOCK, inner), F32),
                    pltpu.VMEM((4, rows, inner), F32),
                    pltpu.VMEM((2, rows, inner), F32),
                    pltpu.SemaphoreType.DMA((len(inputs),)),
                    pltpu.SemaphoreType.DMA,
                ],
                compiler_params=pltpu.CompilerParams(vmem_limit_bytes=VMEM_BYTES),
                cost_estimate=pl.CostEstimate(
                    flops=10**10, bytes_accessed=50 * 2**20, transcendentals=2**22
                ),
                name="mixer",
            )(here, complement, *inputs)
        )
    line, across_plane, mixed = lax.optimization_barrier((line, across_plane, mixed))
    pieces = [line, *across_plane]
    sets = [(pieces, 0)]
    mask = 1
    while mask < sides:
        sets = sets + [([swap(x, "batch", mask) for x in found], s ^ mask) for found, s in sets]
        mask *= 2

    def project(found, flip, mixed, out):
        operands = (here, side, mixed, *found) + (() if out is None else (out,))
        return pl.pallas_call(
            partial(output_kernel, depth, places, flip),
            out_shape=jax.ShapeDtypeStruct((rows, columns * sides), BF16),
            in_specs=[smem(), smem()] + [hbm()] * (len(operands) - 2),
            out_specs=hbm(),
            scratch_shapes=[
                pltpu.VMEM((depth * count, columns), BF16),
                pltpu.VMEM((rows, inner), BF16),
                pltpu.VMEM((rows, columns), BF16),
                pltpu.SemaphoreType.DMA((count + 1,)),
                pltpu.SemaphoreType.DMA,
            ],
            input_output_aliases={} if out is None else {len(operands) - 1: 0},
            compiler_params=pltpu.CompilerParams(vmem_limit_bytes=VMEM_BYTES),
            cost_estimate=pl.CostEstimate(
                flops=2 * rows * inner * columns, bytes_accessed=2**22, transcendentals=0
            ),
            name="output",
        )(*operands)

    results = []
    for genome in range(genomes):
        out = None
        for found, flip in sets:
            out = project(found, flip, mixed[genome], out)
        results.append(out[None])
    return join(*results) if genomes > 1 else results[0]


def solution(mesh):
    placed = (P("batch", "seq"),) + (P(),) * 10 + (P("seq", "batch"),)
    return jax.shard_map(
        on_device, mesh=mesh, in_specs=placed, out_specs=P("batch", "seq", None), check_vma=False
    )
```

```python
from functools import partial

import jax
import jax.numpy as jnp
import ml_dtypes
import numpy as np
from jax import lax
from jax.experimental import pallas as pl
from jax.experimental.pallas import tpu as pltpu
from jax.sharding import PartitionSpec as P

BLOCK = 256
CHUNK = 64
LANES = 128
WIDE = 256
LOG2E = 1.4426950408889634
EPSILON = 1e-05
ORDERS = ((0, 1), (2, 3))
VMEM_BYTES = 64 * 2**20
F32 = jnp.float32
BF16 = jnp.bfloat16

TN = (((0,), (0,)), ((), ()))
NT = (((1,), (1,)), ((), ()))
NN = (((1,), (0,)), ((), ()))


def dot(a, b, dims=NN):
    return lax.dot_general(a, b, dims, preferred_element_type=F32)


def iota(shape, dim):
    return lax.broadcasted_iota(jnp.int32, shape, dim)


def split3(x):
    high = x.astype(BF16)
    rest = x - high.astype(F32)
    middle = rest.astype(BF16)
    low = (rest - middle.astype(F32)).astype(BF16)
    return high, middle, low


def silu(x):
    return x / (1.0 + jnp.exp(-x))


def word_select(letters, taps):
    part = -(-letters * taps // 16) * 16
    codes = np.arange(letters**taps)
    select = np.zeros((len(codes), 4 * part), np.float32)
    last = np.zeros((len(codes), 32), np.float32)
    for back in range(taps):
        letter = codes // letters**back % letters
        for copy in range(3):
            select[codes, copy * part + (taps - 1 - back) * letters + letter] = 1
    select[:, 3 * part : 3 * part + 3] = 1
    for copy in range(2):
        last[codes, copy * 16 + codes % letters] = 1
    return select.astype(ml_dtypes.bfloat16), last.astype(ml_dtypes.bfloat16)


PASSES = ((False, 0, 0), (False, 1, 1), (True, 0, 1), (True, 1, 0))


def letter_rows(table, letters, rows, complement):
    row = iota((rows, 1), 0) % letters
    picked = row
    if complement is not None:
        picked = jnp.zeros_like(row)
        for letter in range(letters):
            picked = jnp.where(row == letter, complement(letter), picked)
    result = jnp.broadcast_to(table[0:1], (rows, table.shape[1]))
    for letter in range(1, letters):
        result = jnp.where(picked == letter, table[letter : letter + 1], result)
    return result


def pack_split(x, copies):
    return jnp.concatenate(split3(x)[:copies], axis=0)


def start_all(pairs, sems):
    copies = [
        pltpu.make_async_copy(source, target, sems.at[k]) for k, (source, target) in enumerate(pairs)
    ]
    for copy in copies:
        copy.start()
    return copies


def word_index(both, start, size, falls, taps, letters, before_end):
    lanes = both.shape[1]
    codes, scale = None, 1
    for back in range(taps):
        turned = both if back == 0 else pltpu.roll(both, lanes - back if falls else back, 1)
        part = scale * turned[:, start : start + size]
        codes = part if codes is None else codes + part
        scale *= letters
    return jnp.where(before_end < taps - 1, scale + before_end, codes)


def first_words(tokens, letters, taps, part, width):
    row, col = iota((16, width), 0), iota((16, width), 1)
    inner_col = col % part
    found = (col >= 3 * part) & (col < 3 * part + 3)
    for length in range(1, taps):
        for back in range(length):
            want = (taps - 1 - back) * letters + tokens[length - 1 - back]
            found = found | ((row == length - 1) & (col < 3 * part) & (inner_col == want))
    return jnp.where(found & (row < taps - 1), 1.0, 0.0).astype(BF16)


def first_last(tokens, letters, taps):
    row, col = iota((16, 32), 0), iota((16, 32), 1) % 16
    found = jnp.zeros((16, 32), jnp.bool_)
    for length in range(1, taps):
        found = found | ((row == length - 1) & (col == tokens[length - 1]))
    return jnp.where(found, 1.0, 0.0).astype(BF16)


def spread_rows(spread, index, count):
    heads = spread.shape[0]
    stacked = jnp.concatenate([spread] * count, axis=0)
    return jnp.where(iota(stacked.shape, 0) // heads == index, stacked, jnp.zeros_like(stacked))


def mixer_kernel(
    letters,
    taps,
    state,
    count,
    here_ref,
    complement_ref,
    *refs,
):
    token_hbms, refs = refs[:4], refs[4:]
    (
        spread_hbm,
        embedding_hbm,
        step_weight_hbm,
        step_bias_hbm,
        rate_hbm,
        skip_hbm,
        last_hbm,
        select_hbm,
        conv_weight_hbm,
        conv_bias_hbm,
        gain_hbm,
        projected_hbm,
        mixed_hbm,
        tokens_ref,
        spread_ref,
        embedding_ref,
        step_weight_ref,
        step_bias_ref,
        rate_ref,
        skip_ref,
        last_ref,
        select_ref,
        conv_weight_ref,
        conv_bias_ref,
        gain_ref,
        projected_ref,
        mixed_ref,
        words_ref,
        gates_ref,
        coefs_ref,
        exponent_ref,
        match_ref,
        weight_ref,
        base_ref,
        gated_ref,
        gate_ref,
        scale_ref,
        in_sems,
        out_sem,
    ) = refs
    reads = start_all(
        (
            *((hbm, tokens_ref.at[k]) for k, hbm in enumerate(token_hbms)),
            (spread_hbm, spread_ref),
            (embedding_hbm, embedding_ref),
            (step_weight_hbm, step_weight_ref),
            (step_bias_hbm, step_bias_ref),
            (rate_hbm, rate_ref),
            (skip_hbm, skip_ref),
            (last_hbm, last_ref),
            (select_hbm, select_ref),
            (conv_weight_hbm, conv_weight_ref),
            (conv_bias_hbm, conv_bias_ref),
            (gain_hbm, gain_ref),
            (projected_hbm, projected_ref),
        ),
        in_sems,
    )
    here = here_ref[0]
    rows = tokens_ref.shape[2]
    own = rows // BLOCK
    blocks = count * own
    heads, inner = spread_ref.shape
    head = inner // heads
    full = select_ref.shape[0]
    part_rows = select_ref.shape[1] // 4
    first, past = here * own, (here + 1) * own
    chunks = BLOCK // CHUNK
    as_bf16 = lambda mask: jnp.where(mask, 1.0, 0.0).astype(BF16)
    complement = lambda letter: complement_ref[letter]

    for copy in reads:
        copy.wait()
    tokens16 = jnp.concatenate([tokens_ref[k] for k in range(4)], axis=0).astype(F32).astype(BF16)
    place, target = iota((blocks, count), 1), iota((blocks, count), 0)
    source = here ^ (place % (count // 4) * 4 + place // (count // 4))
    around = jnp.zeros((3 * blocks, BLOCK), F32)
    for part in range(own):
        block = source * own + part
        pick = jnp.concatenate([as_bf16(block == target + k) for k in (-1, 0, 1)], axis=0)
        around = around + dot(pick, tokens16[:, part * BLOCK : (part + 1) * BLOCK])
    around = around.astype(jnp.int32)
    before, middle, after = (around[k * blocks : (k + 1) * blocks] for k in range(3))
    position = iota((blocks, BLOCK), 0) * BLOCK + iota((blocks, BLOCK), 1)
    rise_index = word_index(
        jnp.concatenate([before, middle], axis=1), BLOCK, BLOCK, False, taps, letters, position
    )
    fall_index = word_index(
        jnp.concatenate([middle, after], axis=1),
        0,
        BLOCK,
        True,
        taps,
        letters,
        blocks * BLOCK - 1 - position,
    )
    block_of = iota((blocks, BLOCK), 0)
    middle_word = full // 2
    word = (iota((full + 16, BLOCK), 0) - middle_word).astype(F32).astype(BF16)
    index = jnp.where(block_of < first, rise_index, fall_index) - middle_word
    index = index.astype(F32).astype(BF16)
    one, zero = jnp.ones((), BF16), jnp.zeros((), BF16)
    for block in range(blocks):
        match_ref[:, block * BLOCK : (block + 1) * BLOCK] = jnp.where(
            word[:full] == index[block : block + 1], one, zero
        )
    ends = [
        jnp.where(word[full:] == index[block : block + 1], one, zero) for block in (0, blocks - 1)
    ]

    end_tokens = (
        [middle[:1, k : k + 1] for k in range(taps - 1)],
        [middle[blocks - 1 :, BLOCK - 1 - k : BLOCK - k] for k in range(taps - 1)],
    )

    letter_hot = [jnp.where(middle == letter, 1.0, 0.0) for letter in range(letters)]
    stack = jnp.concatenate(letter_hot, axis=0).astype(BF16)
    t = iota((BLOCK, BLOCK), 0)
    u = iota((BLOCK, BLOCK), 1)
    sums = dot(stack, jnp.concatenate([as_bf16(t <= u), jnp.ones((BLOCK, BLOCK), BF16)], axis=1))
    running, block_sum = sums[:, :BLOCK], sums[:, BLOCK:].astype(BF16)
    col, row = iota((blocks, blocks), 1), iota((blocks, blocks), 0)
    to_rise = as_bf16((col >= row) & (col < first))
    to_fall = as_bf16((col >= past) & (col < row))
    both_ways = jnp.concatenate([to_rise, to_fall], axis=0)
    counts = []
    for letter in range(letters):
        part = slice(letter * blocks, (letter + 1) * blocks)
        far = dot(both_ways, block_sum[part])
        rise = far[:blocks] - running[part]
        fall = far[blocks:] + running[part] - letter_hot[letter]
        counts.append(jnp.where(block_of < first, rise, fall))

    same = (t // CHUNK) == (u // CHUNK)
    until, since = as_bf16(same & (u <= t)), as_bf16(same & (u >= t))
    half = iota((BLOCK, LANES), 1) % CHUNK
    inside_row = iota((BLOCK, LANES), 0) % CHUNK
    lane = iota((BLOCK, LANES), 1)
    hot_lane = jnp.where(lane < 48, (lane % 16).astype(F32), -1.0)
    word_lane = iota((BLOCK, full), 1).astype(F32)
    end_lane = (iota((16, 16), 1) + full).astype(F32)
    small_half = iota((CHUNK, LANES), 1) % CHUNK
    small_row = iota((CHUNK, LANES), 0)
    small_lane = iota((CHUNK, LANES), 1)
    row_lane = iota((1, LANES), 1)
    beyond = (as_bf16(inside_row > half), as_bf16(inside_row < half))
    row8 = iota((8, BLOCK), 0)
    prepared = []
    for part in range(own):
        mine = block_of == first + part
        take = lambda x: jnp.sum(jnp.where(mine, x, 0), axis=0, keepdims=True)
        token_row = take(middle).astype(F32)
        facts = jnp.where(row8 == 0, take(rise_index), take(fall_index)).astype(F32)
        facts = jnp.where(row8 == 2, token_row, facts)
        facts = jnp.concatenate([facts, jnp.zeros((LANES - 8, BLOCK), F32)], axis=0).T
        matches = [
            jnp.where(word_lane == facts[:, d : d + 1], 1.0, 0.0).astype(BF16) for d in range(2)
        ]
        matches += [
            jnp.where(end_lane == facts[at : at + 16, d : d + 1], 1.0, 0.0).astype(BF16)
            for d, at in ((0, 0), (1, BLOCK - 16))
        ]
        hot = jnp.where(hot_lane == facts[:, 2:3], 1.0, 0.0)
        hot16 = hot.astype(BF16)
        tallies = dot(jnp.concatenate([until, since], axis=0), hot16)
        hot_rows = [jnp.where(token_row == l, 1.0, 0.0) for l in range(letters)]
        between = []
        for d, reach in enumerate((until, since)):
            left = jnp.concatenate([reach * h.astype(BF16) for h in hot_rows], axis=0)
            between.append(dot(left, beyond[d]))
        totals = jnp.concatenate(
            [jnp.where(u[:1] // CHUNK == i, h, 0.0) for i in range(chunks) for h in hot_rows],
            axis=0,
        ).astype(BF16)
        totals = dot(totals, jnp.ones((BLOCK, LANES), BF16))
        doubled = []
        for i in range(chunks):
            window = token_row[:, (i // 2) * LANES : (i // 2 + 1) * LANES]
            keep = (row_lane // CHUNK) == i % 2
            doubled.append(jnp.where(keep, window, pltpu.roll(window, CHUNK, 1)))
        prepared.append((matches, hot, hot16, tallies, between, totals, doubled))

    spread = spread_ref[...]
    width = embedding_ref.shape[1]
    embedding = jnp.concatenate(
        [embedding_ref[...], jnp.zeros((16 - letters, width), BF16)], axis=0
    )
    raw = dot(embedding, step_weight_ref[...], NT)

    def widen(x):
        return sum(dot(piece, spread) for piece in split3(x))

    row = iota((16, heads), 0)
    vectors = jnp.zeros((16, heads), F32)
    for k in range(2):
        vectors = jnp.where(row == k, step_bias_ref[k : k + 1, :], vectors)
        vectors = jnp.where(row == 2 + k, rate_ref[k : k + 1, :], vectors)
        vectors = jnp.where(row == 4 + k, skip_ref[k : k + 1, :], vectors)
    wide_both = widen(jnp.concatenate([raw, vectors], axis=0))
    wide_raw, wide_vectors = wide_both[:16], wide_both[16:]

    def step_tables(raw_rows, vector_rows, strand, param):
        rows8 = letter_rows(raw_rows, letters, 8, complement if strand else None)
        shifted = rows8 + vector_rows[param : param + 1]
        step = jnp.maximum(shifted, 0.0) + jnp.log1p(jnp.exp(-jnp.abs(shifted)))
        decay = -vector_rows[2 + param : 3 + param] * step * LOG2E
        return step, decay, jnp.log2(step)

    lane8 = iota((8, LANES), 1)
    exponents = [jnp.zeros((8, LANES), F32)] * 3
    talls = []
    for index4, (falls, strand, param) in enumerate(PASSES):
        _, decay, log_step = step_tables(wide_raw, wide_vectors, strand, param)
        coefs_ref[index4, 0:8] = decay
        coefs_ref[index4, 8:16] = log_step
        coefs_ref[index4, 16:24] = jnp.broadcast_to(wide_vectors[4 + param : 5 + param], (8, inner))
        step, decay, log_step = step_tables(raw, vectors, strand, param)
        for place, narrow in enumerate((decay, log_step, step)):
            wide = jnp.concatenate([narrow, jnp.zeros((8, LANES - heads), F32)], axis=1)
            wide = pltpu.roll(wide, index4 * heads, 1) if index4 else wide
            mine = (lane8 >= index4 * heads) & (lane8 < (index4 + 1) * heads)
            exponents[place] = jnp.where(mine, wide, exponents[place])
    only = iota((8, LANES), 0) < letters
    tall = jnp.concatenate([exponents[0], jnp.zeros((LANES - 8, LANES), F32)], axis=0).T
    exponents = [
        jnp.concatenate([jnp.where(only, x, 0.0), jnp.zeros((8, LANES), F32)], axis=0)
        for x in exponents
    ]
    for place in range(2):
        rest = jnp.zeros((LANES - 48, LANES), BF16)
        exponent_ref[place] = jnp.concatenate([*split3(exponents[place]), rest], axis=0)
    lasts = [last_ref[...]] + [first_last(x, letters, taps) for x in end_tokens]
    word_steps = dot(jnp.concatenate(lasts, axis=0), pack_split(exponents[2], 2))

    talls = [
        [
            jnp.broadcast_to(tall[k * 2 * heads : (k + 1) * 2 * heads, l : l + 1], (2 * heads, BLOCK))
            for l in range(letters)
        ]
        for k in range(2)
    ]
    for block in range(blocks):
        rises, falls = block < first, block >= past
        power = sum(
            counts[l][block : block + 1] * jnp.where(rises, talls[0][l], talls[1][l])
            for l in range(letters)
        )
        weight = jnp.exp2(power)
        lanes = slice(block * BLOCK, (block + 1) * BLOCK)
        weight_ref[: 2 * heads, lanes] = jnp.where(rises, weight, 0.0).astype(BF16)
        weight_ref[2 * heads :, lanes] = jnp.where(falls, weight, 0.0).astype(BF16)
    word_weights = dot(match_ref[...], weight_ref[...], NT)
    end_weights = [
        dot(end, weight_ref[:, block * BLOCK : (block + 1) * BLOCK], NT)
        for end, block in zip(ends, (0, blocks - 1))
    ]
    word_weights = jnp.concatenate([word_weights, *end_weights], axis=0)
    word_weights = (word_weights * word_steps[:, : 4 * heads]).astype(BF16)
    end_selects = [
        first_words(x, letters, taps, part_rows, 4 * part_rows) for x in end_tokens
    ]

    narrows = []
    for matches, hot, hot16, tallies, between, totals, doubled in prepared:
        up, down = tallies[:BLOCK], tallies[BLOCK:]
        powers = dot(
            jnp.concatenate([up, down, down - hot, up - hot], axis=0).astype(BF16), exponent_ref[0]
        )
        power = lambda k: powers[k * BLOCK : (k + 1) * BLOCK]
        steps = dot(hot16, exponent_ref[1])
        chunk_power = [power(0)[(i + 1) * CHUNK - 1 : (i + 1) * CHUNK] for i in range(chunks)]
        found = []
        for falls in (False, True):
            ends_at = power(2 + falls) + steps
            pieces = [power(int(falls))]
            for i in range(chunks + 1):
                target = chunks - 1 - i if falls else i
                if i == chunks and own == 1:
                    continue
                for j in range(chunks):
                    passed = range(target + 1, j) if falls else range(j + 1, target)
                    if (j > target) if falls else (j < target):
                        pieces.append(
                            ends_at[j * CHUNK : (j + 1) * CHUNK] + sum(chunk_power[m] for m in passed)
                        )
            found.append(jnp.exp2(jnp.concatenate(pieces, axis=0)).astype(BF16)[:, : 4 * heads])
        narrows.append(found)

    projected = projected_ref[...].astype(F32)
    gate = silu(projected[:, :inner])
    for strand in range(2):
        gate_rows = letter_rows(gate, letters, 16, complement if strand else None)
        gate_rows = jnp.where(iota((16, 1), 0) < letters, gate_rows, 0.0)
        gates_ref[strand] = pack_split(gate_rows, 2)

    block_chunk = t // CHUNK
    lane_chunk = u // CHUNK
    head_of = iota((CHUNK, WIDE), 1) // head
    head_masks = [as_bf16(head_of == h) for h in range(WIDE // head)]
    def one_pass(index4):
        falls, strand, param = PASSES[index4]
        d = int(falls)
        inputs = letter_rows(
            projected[:, inner:], letters, part_rows, complement if strand else None
        )
        tap_row = iota((part_rows, 1), 0) // letters
        weights = jnp.zeros((part_rows, inputs.shape[1]), F32)
        for tap in range(taps):
            weights = jnp.where(tap_row == tap, conv_weight_ref[param, tap : tap + 1, :], weights)
        bias_rows = jnp.zeros((part_rows, inputs.shape[1]), F32)
        for place, piece in enumerate(split3(conv_bias_ref[param : param + 1, :])):
            bias_rows = jnp.where(iota((part_rows, 1), 0) == place, piece.astype(F32), bias_rows)
        products = jnp.concatenate([*split3(weights * inputs), bias_rows.astype(BF16)], axis=0)
        select = jnp.concatenate([select_ref[...], end_selects[d]], axis=0)
        conved = silu(dot(select, products))
        yield
        words_ref[index4, :, :inner] = conved[:, :inner].astype(BF16)
        rest = conved[:, inner:]
        rest_lane = iota(rest.shape, 1)
        words_ref[index4, :, inner : inner + LANES] = jnp.where(
            rest_lane < state, pltpu.roll(rest, LANES - state, 1), 0.0
        ).astype(BF16)
        turned = rest.T[:state].astype(BF16)
        to_lanes = spread_rows(spread, index4, 4)
        yield
        own_weights = jnp.concatenate(
            [word_weights[:full], word_weights[full + 16 * d : full + 16 * (d + 1)]], axis=0
        )
        weighted = (dot(own_weights, to_lanes) * conved[:, :inner]).astype(BF16)
        held = dot(turned, weighted)

        yield
        decay = [coefs_ref[index4, l : l + 1] for l in range(letters)]
        log_step = [coefs_ref[index4, 8 + l : 9 + l] for l in range(letters)]
        skip = coefs_ref[index4, 16:17]
        squares = []
        for part in range(own - 1, -1, -1) if falls else range(own):
            matches, _, hot16, _, between, totals, doubled = prepared[part]
            match, end_match, at = matches[d], matches[2 + d], part * BLOCK

            def looked_up(columns):
                found = dot(match, words_ref[index4, :full, columns])
                more = dot(end_match, words_ref[index4, full:, columns])
                if falls:
                    return jnp.concatenate([found[: BLOCK - 16], found[BLOCK - 16 :] + more], axis=0)
                return jnp.concatenate([found[:16] + more, found[16:]], axis=0)

            order = range(chunks - 1, -1, -1) if falls else range(chunks)
            end_bt = dot(turned[:, full:], end_match, NT)
            bt = dot(turned[:, :full], match, NT)
            if falls:
                bt = jnp.concatenate([bt[:, : BLOCK - 16], bt[:, BLOCK - 16 :] + end_bt], axis=1)
            else:
                bt = jnp.concatenate([bt[:, :16] + end_bt, bt[:, 16:]], axis=1)
            c_rows = looked_up(slice(inner, inner + LANES))
            values = looked_up(slice(0, inner))
            yield
            spreads = dot(narrows[part][d], to_lanes)
            yield
            c16, bt16 = c_rows.astype(BF16)[:, :state], bt.astype(BF16)
            all_scores = dot(c16, bt16)
            values16 = values.astype(BF16)
            scores = []
            for i in range(chunks):
                lanes = slice((i // 2) * LANES, (i // 2 + 1) * LANES)
                window = all_scores[i * CHUNK : (i + 1) * CHUNK, lanes]
                keep = (small_lane // CHUNK) == i % 2
                both = jnp.where(keep, window, pltpu.roll(window, CHUNK, 1))
                causal = (small_half >= small_row) if falls else (small_half <= small_row)
                scores.append(jnp.where(causal, both, 0.0))
            yield
            twice = c_rows + pltpu.roll(c_rows, state, 1)
            c_chunks = jnp.concatenate([twice] * (chunks * state // LANES), axis=1)
            earlier = (lane_chunk > block_chunk) if falls else (lane_chunk < block_chunk)
            left = jnp.where(earlier, all_scores, 0.0)
            left = jnp.where(lane_chunk == block_chunk, c_chunks, left).astype(BF16)
            used = BLOCK
            power_sum = None
            pairs = LANES // CHUNK
            for i in order:
                decayed = held if power_sum is None else held * jnp.exp2(power_sum)
                blocks_of = [jnp.zeros((CHUNK, inner), BF16)] * chunks
                blocks_of[i] = decayed.astype(BF16)
                others = range(i + 1, chunks) if falls else range(i)
                for j in others:
                    rows_of = slice(j * CHUNK, (j + 1) * CHUNK)
                    blocks_of[j] = (values[rows_of] * spreads[used : used + CHUNK]).astype(BF16)
                    used += CHUNK
                low = (i // pairs) * pairs if falls else 0
                high = chunks if falls else (i // pairs + 1) * pairs
                chunk = slice(i * CHUNK, (i + 1) * CHUNK)
                carried = dot(
                    left[chunk, low * CHUNK : high * CHUNK],
                    jnp.concatenate(blocks_of[low:high], axis=0),
                )
                base_ref[index4, chunk] = carried * spreads[chunk] + skip * values[chunk]
                for l in range(letters):
                    row = totals[i * letters + l : i * letters + l + 1]
                    row = jnp.concatenate([row] * (inner // LANES), axis=1) * decay[l]
                    power_sum = row if power_sum is None else power_sum + row
            if own > 1:
                fresh = dot(bt16, (values * spreads[used : used + BLOCK]).astype(BF16))
                held = held * jnp.exp2(power_sum) + fresh
            yield
            square = [None] * chunks
            for group in range(inner // WIDE):
                wide = slice(group * WIDE, (group + 1) * WIDE)
                mixed, stacked = [], []
                for i in range(chunks):
                    mixing = []
                    for tile in range(WIDE // LANES):
                        low = group * WIDE + tile * LANES
                        lanes = slice(low, low + LANES)
                        total = log_step[0][:, lanes]
                        for l in range(1, letters):
                            total = jnp.where(doubled[i] == l, log_step[l][:, lanes], total)
                        for l in range(letters):
                            apart = between[d][l * BLOCK + i * CHUNK : l * BLOCK + (i + 1) * CHUNK]
                            total = total + apart * decay[l][:, lanes]
                        mixing.append((jnp.exp2(total) * scores[i]).astype(BF16))
                    mixed.append(jnp.concatenate(mixing, axis=1))
                    chunk_values = values16[i * CHUNK : (i + 1) * CHUNK, wide]
                    stacked.append(
                        jnp.concatenate([chunk_values * mask for mask in head_masks], axis=0)
                    )
                yield
                inside = [dot(m, v) for m, v in zip(mixed, stacked)]
                if index4 == strand:
                    gate_ref[strand, at : at + BLOCK, wide] = dot(
                        hot16[:, :32], gates_ref[strand, :, wide]
                    )
                gate = gate_ref[strand, at : at + BLOCK, wide]
                for i in range(chunks):
                    chunk = slice(i * CHUNK, (i + 1) * CHUNK)
                    gated = (inside[i] + base_ref[index4, chunk, wide]) * gate[chunk]
                    gated_ref[index4, at + i * CHUNK : at + (i + 1) * CHUNK, wide] = gated
                    part_sum = jnp.sum(gated * gated, axis=1, keepdims=True)
                    square[i] = part_sum if square[i] is None else square[i] + part_sum
            squares.append(jnp.concatenate(square, axis=0))
        squares = squares[::-1] if falls else squares
        scale = lax.rsqrt(jnp.concatenate(squares, axis=0) * (1.0 / inner) + EPSILON)
        scale_ref[index4] = jnp.broadcast_to(scale, (rows, LANES))

    def run(orders):
        live = [one_pass(index4) for index4 in orders]
        while live:
            live = [p for p in live if next(p, live) is not live]

    for orders in ORDERS:
        run(orders)
    writes = []
    for piece in range(rows // CHUNK):
        at = slice(piece * CHUNK, (piece + 1) * CHUNK)
        for tile in range(inner // LANES):
            wide = slice(tile * LANES, (tile + 1) * LANES)
            total = 0.0
            for param in range(2):
                part = sum(
                    gated_ref[k, at, wide] * scale_ref[k, at]
                    for k in range(len(PASSES))
                    if PASSES[k][2] == param
                )
                total = total + part * gain_ref[param : param + 1, wide]
            mixed_ref[at, wide] = total.astype(BF16)
        writes += start_all(
            [(mixed_ref.at[at], mixed_hbm.at[at])], out_sem.at[pl.ds(piece, 1)]
        )
    for copy in writes:
        copy.wait()


def join_kernel(count, *refs):
    total = sum(count)
    pieces, outs = refs[:total], refs[total : total + len(count)]
    held, (in_sems, out_sems) = refs[total + len(count) : -2], refs[-2:]
    pairs = []
    for n, buffer in zip(count, held):
        at = 0
        for piece in pieces[:n]:
            pairs.append((piece, buffer.at[pl.ds(at, piece.shape[0])]))
            at += piece.shape[0]
        pieces = pieces[n:]
    for copy in start_all(pairs, in_sems):
        copy.wait()
    for copy in start_all(list(zip(held, outs)), out_sems):
        copy.wait()


def join_all(*groups):
    shapes = [
        ((sum(x.shape[0] for x in group), *group[0].shape[1:]), group[0].dtype) for group in groups
    ]
    pieces = [x for group in groups for x in group]
    return pl.pallas_call(
        partial(join_kernel, [len(group) for group in groups]),
        out_shape=[jax.ShapeDtypeStruct(*shape) for shape in shapes],
        in_specs=[pl.BlockSpec(memory_space=pl.ANY)] * len(pieces),
        out_specs=[pl.BlockSpec(memory_space=pl.ANY)] * len(shapes),
        scratch_shapes=[pltpu.VMEM(*shape) for shape in shapes]
        + [pltpu.SemaphoreType.DMA((len(pieces),)), pltpu.SemaphoreType.DMA((len(shapes),))],
        compiler_params=pltpu.CompilerParams(vmem_limit_bytes=4 * 2**20),
        name="join",
    )(*pieces)


def output_kernel(depth, places, flip, here_ref, side_ref, mixed_hbm, *refs):
    pieces = refs[: len(places)]
    out_hbm, weight_ref, mixed_ref, out_ref, sem, out_sem = refs[-6:]
    here, side = here_ref[0], side_ref[0]
    pairs = [(mixed_hbm, mixed_ref)]
    for piece, masks in zip(pieces, places):
        for k, mask in enumerate(masks):
            row = pl.multiple_of((here ^ mask) * depth, depth)
            pairs.append((piece.at[k], weight_ref.at[pl.ds(row, depth)]))
    for copy in start_all(pairs, sem):
        copy.wait()
    out_ref[...] = dot(mixed_ref[...], weight_ref[...]).astype(BF16)
    columns = out_ref.shape[1]
    lane = pl.multiple_of((side ^ flip) * columns, columns)
    copy = pltpu.make_async_copy(out_ref, out_hbm.at[:, pl.ds(lane, columns)], out_sem)
    copy.start()
    copy.wait()


def swap(x, axis, mask):
    count = lax.axis_size(axis)
    return lax.ppermute(x, axis, [(i, i ^ mask) for i in range(count)])


def vmem():
    return pl.BlockSpec(memory_space=pltpu.VMEM)


def hbm():
    return pl.BlockSpec(memory_space=pltpu.HBM)


def smem():
    return pl.BlockSpec(memory_space=pltpu.SMEM)


def on_device(
    token_ids,
    complement,
    embedding,
    in_weight,
    step_weight,
    conv_weight,
    conv_bias,
    step_bias,
    decay_rate,
    skip_gain,
    norm_gain,
    out_weight,
):
    genomes, rows = token_ids.shape
    letters, width = embedding.shape
    taps = conv_weight.shape[1]
    heads = step_weight.shape[1]
    inner = norm_gain.shape[1]
    state = (conv_weight.shape[2] - inner) // 2
    count, sides = lax.axis_size("seq"), lax.axis_size("batch")
    here = lax.axis_index("seq").astype(jnp.int32)[None]
    side = lax.axis_index("batch").astype(jnp.int32)[None]
    depth, columns = out_weight.shape

    join = lambda *x: jnp.concatenate(x, axis=0)
    moved = lambda masks, mask: [m ^ mask for m in masks]
    line, line_masks = out_weight[None], [0]
    tokens = token_ids[None]
    token_line = [swap(tokens, "seq", mask) for mask in range(count - 4, 0, -4)]
    mask = count // 2
    while mask > 2:
        arrived = swap(line, "seq", mask)
        if mask == count // 2:
            projected = jnp.dot(embedding, in_weight, preferred_element_type=F32).astype(BF16)
            arrived, token_line, projected = lax.optimization_barrier(
                (arrived, token_line, projected)
            )
            line, token_line = join_all((line, arrived), (tokens, *token_line[::-1]))
            tokens = [token_line] + [swap(token_line, "seq", m) for m in (1, 2, 3)]
        else:
            (line,) = join_all((line, arrived))
        line_masks = line_masks + moved(line_masks, mask)
        mask //= 2
    across_plane = [swap(line, "seq", mask) for mask in (1, 2, 3)]
    places = [line_masks] + [moved(line_masks, mask) for mask in (1, 2, 3)]

    select, last = word_select(letters, taps)
    word_rows = select.shape[0]
    spread = np.repeat(np.eye(heads, dtype=np.float32), inner // heads, axis=1).astype(
        ml_dtypes.bfloat16
    )
    mixed = []
    for genome in range(genomes):
        inputs = (
            *(x[:, genome] for x in tokens),
            spread,
            embedding,
            step_weight.T,
            step_bias,
            decay_rate,
            skip_gain,
            last,
            select,
            conv_weight,
            conv_bias,
            norm_gain,
            projected,
        )
        mixed.append(
            pl.pallas_call(
                partial(mixer_kernel, letters, taps, state, count),
                out_shape=jax.ShapeDtypeStruct((rows, inner), BF16),
                in_specs=[smem(), smem()] + [hbm()] * len(inputs),
                out_specs=hbm(),
                scratch_shapes=[pltpu.VMEM((4, *inputs[0].shape), jnp.int32)]
                + [pltpu.VMEM(x.shape, x.dtype) for x in inputs[4:]]
                + [
                    pltpu.VMEM((rows, inner), BF16),
                    pltpu.VMEM((4, word_rows + 16, inner + LANES), BF16),
                    pltpu.VMEM((2, 32, inner), BF16),
                    pltpu.VMEM((4, 24, inner), F32),
                    pltpu.VMEM((2, LANES, LANES), BF16),
                    pltpu.VMEM((letters**taps, count * rows), BF16),
                    pltpu.VMEM((4 * heads, count * rows), BF16),
                    pltpu.VMEM((4, BLOCK, inner), F32),
                    pltpu.VMEM((4, rows, inner), F32),
                    pltpu.VMEM((2, rows, inner), F32),
                    pltpu.VMEM((4, rows, LANES), F32),
                    pltpu.SemaphoreType.DMA((len(inputs),)),
                    pltpu.SemaphoreType.DMA((rows // CHUNK,)),
                ],
                compiler_params=pltpu.CompilerParams(vmem_limit_bytes=VMEM_BYTES),
                cost_estimate=pl.CostEstimate(
                    flops=10**10, bytes_accessed=50 * 2**20, transcendentals=2**22
                ),
                name="mixer",
            )(here, complement, *inputs)
        )
    line, across_plane, mixed = lax.optimization_barrier((line, across_plane, mixed))
    pieces = [line, *across_plane]
    sets = [(pieces, 0)]
    mask = 1
    while mask < sides:
        sets = sets + [([swap(x, "batch", mask) for x in found], s ^ mask) for found, s in sets]
        mask *= 2

    def project(found, flip, mixed, out):
        operands = (here, side, mixed, *found) + (() if out is None else (out,))
        return pl.pallas_call(
            partial(output_kernel, depth, places, flip),
            out_shape=jax.ShapeDtypeStruct((rows, columns * sides), BF16),
            in_specs=[smem(), smem()] + [hbm()] * (len(operands) - 2),
            out_specs=hbm(),
            scratch_shapes=[
                pltpu.VMEM((depth * count, columns), BF16),
                pltpu.VMEM((rows, inner), BF16),
                pltpu.VMEM((rows, columns), BF16),
                pltpu.SemaphoreType.DMA((count + 1,)),
                pltpu.SemaphoreType.DMA,
            ],
            input_output_aliases={} if out is None else {len(operands) - 1: 0},
            compiler_params=pltpu.CompilerParams(vmem_limit_bytes=VMEM_BYTES),
            cost_estimate=pl.CostEstimate(
                flops=2 * rows * inner * columns, bytes_accessed=2**22, transcendentals=0
            ),
            name="output",
        )(*operands)

    results = []
    for genome in range(genomes):
        out = None
        for found, flip in sets:
            out = project(found, flip, mixed[genome], out)
        results.append(out[None])
    return join(*results) if genomes > 1 else results[0]


def solution(mesh):
    placed = (P("batch", "seq"),) + (P(),) * 10 + (P("seq", "batch"),)
    return jax.shard_map(
        on_device, mesh=mesh, in_specs=placed, out_specs=P("batch", "seq", None), check_vma=False
    )
```

```python
from functools import partial

import jax
import jax.numpy as jnp
import ml_dtypes
import numpy as np
from jax import lax
from jax.experimental import pallas as pl
from jax.experimental.pallas import tpu as pltpu
from jax.sharding import PartitionSpec as P

BLOCK = 256
CHUNK = 64
LANES = 128
WIDE = 256
LOG2E = 1.4426950408889634
EPSILON = 1e-05
ORDERS = ((0, 1), (2, 3))
VMEM_BYTES = 36 * 2**20
F32 = jnp.float32
BF16 = jnp.bfloat16

TN = (((0,), (0,)), ((), ()))
NT = (((1,), (1,)), ((), ()))
NN = (((1,), (0,)), ((), ()))


def dot(a, b, dims=NN):
    return lax.dot_general(a, b, dims, preferred_element_type=F32)


def iota(shape, dim):
    return lax.broadcasted_iota(jnp.int32, shape, dim)


def split3(x):
    high = x.astype(BF16)
    rest = x - high.astype(F32)
    middle = rest.astype(BF16)
    low = (rest - middle.astype(F32)).astype(BF16)
    return high, middle, low


def silu(x):
    return x / (1.0 + jnp.exp(-x))


def word_select(letters, taps):
    part = -(-letters * taps // 16) * 16
    codes = np.arange(letters**taps)
    select = np.zeros((len(codes), 4 * part), np.float32)
    last = np.zeros((len(codes), 32), np.float32)
    for back in range(taps):
        letter = codes // letters**back % letters
        for copy in range(3):
            select[codes, copy * part + (taps - 1 - back) * letters + letter] = 1
    select[:, 3 * part : 3 * part + 3] = 1
    for copy in range(2):
        last[codes, copy * 16 + codes % letters] = 1
    return select.astype(ml_dtypes.bfloat16), last.astype(ml_dtypes.bfloat16)


PASSES = ((False, 0, 0), (False, 1, 1), (True, 0, 1), (True, 1, 0))


def letter_rows(table, letters, rows, complement):
    row = iota((rows, 1), 0) % letters
    picked = row
    if complement is not None:
        picked = jnp.zeros_like(row)
        for letter in range(letters):
            picked = jnp.where(row == letter, complement(letter), picked)
    result = jnp.broadcast_to(table[0:1], (rows, table.shape[1]))
    for letter in range(1, letters):
        result = jnp.where(picked == letter, table[letter : letter + 1], result)
    return result


def pack_split(x, copies):
    return jnp.concatenate(split3(x)[:copies], axis=0)


def start_all(pairs, sems):
    copies = [
        pltpu.make_async_copy(source, target, sems.at[k]) for k, (source, target) in enumerate(pairs)
    ]
    for copy in copies:
        copy.start()
    return copies


def word_index(both, start, size, falls, taps, letters, before_end):
    lanes = both.shape[1]
    codes, scale = None, 1
    for back in range(taps):
        turned = both if back == 0 else pltpu.roll(both, lanes - back if falls else back, 1)
        part = scale * turned[:, start : start + size]
        codes = part if codes is None else codes + part
        scale *= letters
    return jnp.where(before_end < taps - 1, scale + before_end, codes)


def first_words(tokens, letters, taps, part, width):
    row, col = iota((16, width), 0), iota((16, width), 1)
    inner_col = col % part
    found = (col >= 3 * part) & (col < 3 * part + 3)
    for length in range(1, taps):
        for back in range(length):
            want = (taps - 1 - back) * letters + tokens[length - 1 - back]
            found = found | ((row == length - 1) & (col < 3 * part) & (inner_col == want))
    return jnp.where(found & (row < taps - 1), 1.0, 0.0).astype(BF16)


def first_last(tokens, letters, taps):
    row, col = iota((16, 32), 0), iota((16, 32), 1) % 16
    found = jnp.zeros((16, 32), jnp.bool_)
    for length in range(1, taps):
        found = found | ((row == length - 1) & (col == tokens[length - 1]))
    return jnp.where(found, 1.0, 0.0).astype(BF16)


def spread_rows(spread, index, count):
    heads = spread.shape[0]
    stacked = jnp.concatenate([spread] * count, axis=0)
    return jnp.where(iota(stacked.shape, 0) // heads == index, stacked, jnp.zeros_like(stacked))


def mixer_kernel(
    letters,
    taps,
    state,
    count,
    here_ref,
    complement_ref,
    *refs,
):
    token_refs, refs = refs[:4], refs[4:]
    (
        spread_ref,
        embedding_ref,
        step_weight_ref,
        step_bias_ref,
        rate_ref,
        skip_ref,
        last_ref,
        select_ref,
        conv_weight_ref,
        conv_bias_ref,
        gain_ref,
        projected_ref,
        mixed_ref,
        words_ref,
        gates_ref,
        coefs_ref,
        exponent_ref,
        match_ref,
        weight_ref,
        base_ref,
        gated_ref,
        gate_ref,
        scale_ref,
    ) = refs
    here = here_ref[0]
    rows = mixed_ref.shape[0]
    own = rows // BLOCK
    blocks = count * own
    heads, inner = spread_ref.shape
    head = inner // heads
    full = select_ref.shape[0]
    part_rows = select_ref.shape[1] // 4
    first, past = here * own, (here + 1) * own
    chunks = BLOCK // CHUNK
    as_bf16 = lambda mask: jnp.where(mask, 1.0, 0.0).astype(BF16)
    complement = lambda letter: complement_ref[letter]

    tokens16 = jnp.concatenate([ref[...] for ref in token_refs], axis=0).astype(F32).astype(BF16)
    place, target = iota((blocks, count), 1), iota((blocks, count), 0)
    source = here ^ (place % (count // 4) * 4 + place // (count // 4))
    around = jnp.zeros((3 * blocks, BLOCK), F32)
    for part in range(own):
        block = source * own + part
        pick = jnp.concatenate([as_bf16(block == target + k) for k in (-1, 0, 1)], axis=0)
        around = around + dot(pick, tokens16[:, part * BLOCK : (part + 1) * BLOCK])
    around = around.astype(jnp.int32)
    before, middle, after = (around[k * blocks : (k + 1) * blocks] for k in range(3))
    position = iota((blocks, BLOCK), 0) * BLOCK + iota((blocks, BLOCK), 1)
    rise_index = word_index(
        jnp.concatenate([before, middle], axis=1), BLOCK, BLOCK, False, taps, letters, position
    )
    fall_index = word_index(
        jnp.concatenate([middle, after], axis=1),
        0,
        BLOCK,
        True,
        taps,
        letters,
        blocks * BLOCK - 1 - position,
    )
    block_of = iota((blocks, BLOCK), 0)
    middle_word = full // 2
    word = (iota((full + 16, BLOCK), 0) - middle_word).astype(F32).astype(BF16)
    index = jnp.where(block_of < first, rise_index, fall_index) - middle_word
    index = index.astype(F32).astype(BF16)
    one, zero = jnp.ones((), BF16), jnp.zeros((), BF16)
    for block in range(blocks):
        match_ref[:, block * BLOCK : (block + 1) * BLOCK] = jnp.where(
            word[:full] == index[block : block + 1], one, zero
        )
    ends = [
        jnp.where(word[full:] == index[block : block + 1], one, zero) for block in (0, blocks - 1)
    ]

    end_tokens = (
        [middle[:1, k : k + 1] for k in range(taps - 1)],
        [middle[blocks - 1 :, BLOCK - 1 - k : BLOCK - k] for k in range(taps - 1)],
    )

    letter_hot = [jnp.where(middle == letter, 1.0, 0.0) for letter in range(letters)]
    stack = jnp.concatenate(letter_hot, axis=0).astype(BF16)
    t = iota((BLOCK, BLOCK), 0)
    u = iota((BLOCK, BLOCK), 1)
    sums = dot(stack, jnp.concatenate([as_bf16(t <= u), jnp.ones((BLOCK, BLOCK), BF16)], axis=1))
    running, block_sum = sums[:, :BLOCK], sums[:, BLOCK:].astype(BF16)
    col, row = iota((blocks, blocks), 1), iota((blocks, blocks), 0)
    to_rise = as_bf16((col >= row) & (col < first))
    to_fall = as_bf16((col >= past) & (col < row))
    both_ways = jnp.concatenate([to_rise, to_fall], axis=0)
    counts = []
    for letter in range(letters):
        part = slice(letter * blocks, (letter + 1) * blocks)
        far = dot(both_ways, block_sum[part])
        rise = far[:blocks] - running[part]
        fall = far[blocks:] + running[part] - letter_hot[letter]
        counts.append(jnp.where(block_of < first, rise, fall))

    same = (t // CHUNK) == (u // CHUNK)
    until, since = as_bf16(same & (u <= t)), as_bf16(same & (u >= t))
    half = iota((BLOCK, LANES), 1) % CHUNK
    inside_row = iota((BLOCK, LANES), 0) % CHUNK
    lane = iota((BLOCK, LANES), 1)
    hot_lane = jnp.where(lane < 48, (lane % 16).astype(F32), -1.0)
    word_lane = iota((BLOCK, full), 1).astype(F32)
    end_lane = (iota((16, 16), 1) + full).astype(F32)
    small_half = iota((CHUNK, LANES), 1) % CHUNK
    small_row = iota((CHUNK, LANES), 0)
    small_lane = iota((CHUNK, LANES), 1)
    row_lane = iota((1, LANES), 1)
    beyond = (as_bf16(inside_row > half), as_bf16(inside_row < half))
    row8 = iota((8, BLOCK), 0)
    prepared = []
    for part in range(own):
        mine = block_of == first + part
        take = lambda x: jnp.sum(jnp.where(mine, x, 0), axis=0, keepdims=True)
        token_row = take(middle).astype(F32)
        facts = jnp.where(row8 == 0, take(rise_index), take(fall_index)).astype(F32)
        facts = jnp.where(row8 == 2, token_row, facts)
        facts = jnp.concatenate([facts, jnp.zeros((LANES - 8, BLOCK), F32)], axis=0).T
        matches = [
            jnp.where(word_lane == facts[:, d : d + 1], 1.0, 0.0).astype(BF16) for d in range(2)
        ]
        matches += [
            jnp.where(end_lane == facts[at : at + 16, d : d + 1], 1.0, 0.0).astype(BF16)
            for d, at in ((0, 0), (1, BLOCK - 16))
        ]
        hot = jnp.where(hot_lane == facts[:, 2:3], 1.0, 0.0)
        hot16 = hot.astype(BF16)
        tallies = dot(jnp.concatenate([until, since], axis=0), hot16)
        hot_rows = [jnp.where(token_row == l, 1.0, 0.0) for l in range(letters)]
        between = []
        for d, reach in enumerate((until, since)):
            left = jnp.concatenate([reach * h.astype(BF16) for h in hot_rows], axis=0)
            between.append(dot(left, beyond[d]))
        totals = jnp.concatenate(
            [jnp.where(u[:1] // CHUNK == i, h, 0.0) for i in range(chunks) for h in hot_rows],
            axis=0,
        ).astype(BF16)
        totals = dot(totals, jnp.ones((BLOCK, LANES), BF16))
        doubled = []
        for i in range(chunks):
            window = token_row[:, (i // 2) * LANES : (i // 2 + 1) * LANES]
            keep = (row_lane // CHUNK) == i % 2
            doubled.append(jnp.where(keep, window, pltpu.roll(window, CHUNK, 1)))
        prepared.append((matches, hot, hot16, tallies, between, totals, doubled))

    spread = spread_ref[...]
    width = embedding_ref.shape[1]
    embedding = jnp.concatenate(
        [embedding_ref[...], jnp.zeros((16 - letters, width), BF16)], axis=0
    )
    raw = dot(embedding, step_weight_ref[...], NT)

    def widen(x):
        return sum(dot(piece, spread) for piece in split3(x))

    row = iota((16, heads), 0)
    vectors = jnp.zeros((16, heads), F32)
    for k in range(2):
        vectors = jnp.where(row == k, step_bias_ref[k : k + 1, :], vectors)
        vectors = jnp.where(row == 2 + k, rate_ref[k : k + 1, :], vectors)
        vectors = jnp.where(row == 4 + k, skip_ref[k : k + 1, :], vectors)
    wide_both = widen(jnp.concatenate([raw, vectors], axis=0))
    wide_raw, wide_vectors = wide_both[:16], wide_both[16:]

    def step_tables(raw_rows, vector_rows, strand, param):
        rows8 = letter_rows(raw_rows, letters, 8, complement if strand else None)
        shifted = rows8 + vector_rows[param : param + 1]
        step = jnp.maximum(shifted, 0.0) + jnp.log1p(jnp.exp(-jnp.abs(shifted)))
        decay = -vector_rows[2 + param : 3 + param] * step * LOG2E
        return step, decay, jnp.log2(step)

    lane8 = iota((8, LANES), 1)
    exponents = [jnp.zeros((8, LANES), F32)] * 3
    talls = []
    for index4, (falls, strand, param) in enumerate(PASSES):
        _, decay, log_step = step_tables(wide_raw, wide_vectors, strand, param)
        coefs_ref[index4, 0:8] = decay
        coefs_ref[index4, 8:16] = log_step
        coefs_ref[index4, 16:24] = jnp.broadcast_to(wide_vectors[4 + param : 5 + param], (8, inner))
        step, decay, log_step = step_tables(raw, vectors, strand, param)
        for place, narrow in enumerate((decay, log_step, step)):
            wide = jnp.concatenate([narrow, jnp.zeros((8, LANES - heads), F32)], axis=1)
            wide = pltpu.roll(wide, index4 * heads, 1) if index4 else wide
            mine = (lane8 >= index4 * heads) & (lane8 < (index4 + 1) * heads)
            exponents[place] = jnp.where(mine, wide, exponents[place])
    only = iota((8, LANES), 0) < letters
    tall = jnp.concatenate([exponents[0], jnp.zeros((LANES - 8, LANES), F32)], axis=0).T
    exponents = [
        jnp.concatenate([jnp.where(only, x, 0.0), jnp.zeros((8, LANES), F32)], axis=0)
        for x in exponents
    ]
    for place in range(2):
        rest = jnp.zeros((LANES - 48, LANES), BF16)
        exponent_ref[place] = jnp.concatenate([*split3(exponents[place]), rest], axis=0)
    lasts = [last_ref[...]] + [first_last(x, letters, taps) for x in end_tokens]
    word_steps = dot(jnp.concatenate(lasts, axis=0), pack_split(exponents[2], 2))

    talls = [
        [
            jnp.broadcast_to(tall[k * 2 * heads : (k + 1) * 2 * heads, l : l + 1], (2 * heads, BLOCK))
            for l in range(letters)
        ]
        for k in range(2)
    ]
    for block in range(blocks):
        rises, falls = block < first, block >= past
        power = sum(
            counts[l][block : block + 1] * jnp.where(rises, talls[0][l], talls[1][l])
            for l in range(letters)
        )
        weight = jnp.exp2(power)
        lanes = slice(block * BLOCK, (block + 1) * BLOCK)
        weight_ref[: 2 * heads, lanes] = jnp.where(rises, weight, 0.0).astype(BF16)
        weight_ref[2 * heads :, lanes] = jnp.where(falls, weight, 0.0).astype(BF16)
    word_weights = dot(match_ref[...], weight_ref[...], NT)
    end_weights = [
        dot(end, weight_ref[:, block * BLOCK : (block + 1) * BLOCK], NT)
        for end, block in zip(ends, (0, blocks - 1))
    ]
    word_weights = jnp.concatenate([word_weights, *end_weights], axis=0)
    word_weights = (word_weights * word_steps[:, : 4 * heads]).astype(BF16)
    end_selects = [
        first_words(x, letters, taps, part_rows, 4 * part_rows) for x in end_tokens
    ]

    narrows = []
    for matches, hot, hot16, tallies, between, totals, doubled in prepared:
        up, down = tallies[:BLOCK], tallies[BLOCK:]
        powers = dot(
            jnp.concatenate([up, down, down - hot, up - hot], axis=0).astype(BF16), exponent_ref[0]
        )
        power = lambda k: powers[k * BLOCK : (k + 1) * BLOCK]
        steps = dot(hot16, exponent_ref[1])
        chunk_power = [power(0)[(i + 1) * CHUNK - 1 : (i + 1) * CHUNK] for i in range(chunks)]
        found = []
        for falls in (False, True):
            ends_at = power(2 + falls) + steps
            pieces = [power(int(falls))]
            for i in range(chunks + 1):
                target = chunks - 1 - i if falls else i
                if i == chunks and own == 1:
                    continue
                for j in range(chunks):
                    passed = range(target + 1, j) if falls else range(j + 1, target)
                    if (j > target) if falls else (j < target):
                        pieces.append(
                            ends_at[j * CHUNK : (j + 1) * CHUNK] + sum(chunk_power[m] for m in passed)
                        )
            found.append(jnp.exp2(jnp.concatenate(pieces, axis=0)).astype(BF16)[:, : 4 * heads])
        narrows.append(found)

    projected = projected_ref[...].astype(F32)
    gate = silu(projected[:, :inner])
    for strand in range(2):
        gate_rows = letter_rows(gate, letters, 16, complement if strand else None)
        gate_rows = jnp.where(iota((16, 1), 0) < letters, gate_rows, 0.0)
        gates_ref[strand] = pack_split(gate_rows, 2)

    block_chunk = t // CHUNK
    lane_chunk = u // CHUNK
    head_of = iota((CHUNK, WIDE), 1) // head
    head_masks = [as_bf16(head_of == h) for h in range(WIDE // head)]
    def one_pass(index4):
        falls, strand, param = PASSES[index4]
        d = int(falls)
        inputs = letter_rows(
            projected[:, inner:], letters, part_rows, complement if strand else None
        )
        tap_row = iota((part_rows, 1), 0) // letters
        weights = jnp.zeros((part_rows, inputs.shape[1]), F32)
        for tap in range(taps):
            weights = jnp.where(tap_row == tap, conv_weight_ref[param, tap : tap + 1, :], weights)
        bias_rows = jnp.zeros((part_rows, inputs.shape[1]), F32)
        for place, piece in enumerate(split3(conv_bias_ref[param : param + 1, :])):
            bias_rows = jnp.where(iota((part_rows, 1), 0) == place, piece.astype(F32), bias_rows)
        products = jnp.concatenate([*split3(weights * inputs), bias_rows.astype(BF16)], axis=0)
        select = jnp.concatenate([select_ref[...], end_selects[d]], axis=0)
        conved = silu(dot(select, products))
        yield
        words_ref[index4, :, :inner] = conved[:, :inner].astype(BF16)
        rest = conved[:, inner:]
        rest_lane = iota(rest.shape, 1)
        words_ref[index4, :, inner : inner + LANES] = jnp.where(
            rest_lane < state, pltpu.roll(rest, LANES - state, 1), 0.0
        ).astype(BF16)
        turned = rest.T[:state].astype(BF16)
        to_lanes = spread_rows(spread, index4, 4)
        yield
        own_weights = jnp.concatenate(
            [word_weights[:full], word_weights[full + 16 * d : full + 16 * (d + 1)]], axis=0
        )
        weighted = (dot(own_weights, to_lanes) * conved[:, :inner]).astype(BF16)
        held = dot(turned, weighted)

        yield
        decay = [coefs_ref[index4, l : l + 1] for l in range(letters)]
        log_step = [coefs_ref[index4, 8 + l : 9 + l] for l in range(letters)]
        skip = coefs_ref[index4, 16:17]
        squares = []
        for part in range(own - 1, -1, -1) if falls else range(own):
            matches, _, hot16, _, between, totals, doubled = prepared[part]
            match, end_match, at = matches[d], matches[2 + d], part * BLOCK

            def looked_up(columns):
                found = dot(match, words_ref[index4, :full, columns])
                more = dot(end_match, words_ref[index4, full:, columns])
                if falls:
                    return jnp.concatenate([found[: BLOCK - 16], found[BLOCK - 16 :] + more], axis=0)
                return jnp.concatenate([found[:16] + more, found[16:]], axis=0)

            order = range(chunks - 1, -1, -1) if falls else range(chunks)
            end_bt = dot(turned[:, full:], end_match, NT)
            bt = dot(turned[:, :full], match, NT)
            if falls:
                bt = jnp.concatenate([bt[:, : BLOCK - 16], bt[:, BLOCK - 16 :] + end_bt], axis=1)
            else:
                bt = jnp.concatenate([bt[:, :16] + end_bt, bt[:, 16:]], axis=1)
            c_rows = looked_up(slice(inner, inner + LANES))
            values = looked_up(slice(0, inner))
            yield
            spreads = dot(narrows[part][d], to_lanes)
            yield
            c16, bt16 = c_rows.astype(BF16)[:, :state], bt.astype(BF16)
            all_scores = dot(c16, bt16)
            values16 = values.astype(BF16)
            scores = []
            for i in range(chunks):
                lanes = slice((i // 2) * LANES, (i // 2 + 1) * LANES)
                window = all_scores[i * CHUNK : (i + 1) * CHUNK, lanes]
                keep = (small_lane // CHUNK) == i % 2
                both = jnp.where(keep, window, pltpu.roll(window, CHUNK, 1))
                causal = (small_half >= small_row) if falls else (small_half <= small_row)
                scores.append(jnp.where(causal, both, 0.0))
            yield
            twice = c_rows + pltpu.roll(c_rows, state, 1)
            c_chunks = jnp.concatenate([twice] * (chunks * state // LANES), axis=1)
            earlier = (lane_chunk > block_chunk) if falls else (lane_chunk < block_chunk)
            left = jnp.where(earlier, all_scores, 0.0)
            left = jnp.where(lane_chunk == block_chunk, c_chunks, left).astype(BF16)
            used = BLOCK
            power_sum = None
            pairs = LANES // CHUNK
            for i in order:
                decayed = held if power_sum is None else held * jnp.exp2(power_sum)
                blocks_of = [jnp.zeros((CHUNK, inner), BF16)] * chunks
                blocks_of[i] = decayed.astype(BF16)
                others = range(i + 1, chunks) if falls else range(i)
                for j in others:
                    rows_of = slice(j * CHUNK, (j + 1) * CHUNK)
                    blocks_of[j] = (values[rows_of] * spreads[used : used + CHUNK]).astype(BF16)
                    used += CHUNK
                low = (i // pairs) * pairs if falls else 0
                high = chunks if falls else (i // pairs + 1) * pairs
                chunk = slice(i * CHUNK, (i + 1) * CHUNK)
                carried = dot(
                    left[chunk, low * CHUNK : high * CHUNK],
                    jnp.concatenate(blocks_of[low:high], axis=0),
                )
                base_ref[index4, chunk] = carried * spreads[chunk] + skip * values[chunk]
                for l in range(letters):
                    row = totals[i * letters + l : i * letters + l + 1]
                    row = jnp.concatenate([row] * (inner // LANES), axis=1) * decay[l]
                    power_sum = row if power_sum is None else power_sum + row
            if own > 1:
                fresh = dot(bt16, (values * spreads[used : used + BLOCK]).astype(BF16))
                held = held * jnp.exp2(power_sum) + fresh
            yield
            square = [None] * chunks
            for group in range(inner // WIDE):
                wide = slice(group * WIDE, (group + 1) * WIDE)
                mixed, stacked = [], []
                for i in range(chunks):
                    mixing = []
                    for tile in range(WIDE // LANES):
                        low = group * WIDE + tile * LANES
                        lanes = slice(low, low + LANES)
                        total = log_step[0][:, lanes]
                        for l in range(1, letters):
                            total = jnp.where(doubled[i] == l, log_step[l][:, lanes], total)
                        for l in range(letters):
                            apart = between[d][l * BLOCK + i * CHUNK : l * BLOCK + (i + 1) * CHUNK]
                            total = total + apart * decay[l][:, lanes]
                        mixing.append((jnp.exp2(total) * scores[i]).astype(BF16))
                    mixed.append(jnp.concatenate(mixing, axis=1))
                    chunk_values = values16[i * CHUNK : (i + 1) * CHUNK, wide]
                    stacked.append(
                        jnp.concatenate([chunk_values * mask for mask in head_masks], axis=0)
                    )
                yield
                inside = [dot(m, v) for m, v in zip(mixed, stacked)]
                if index4 == strand:
                    gate_ref[strand, at : at + BLOCK, wide] = dot(
                        hot16[:, :32], gates_ref[strand, :, wide]
                    )
                gate = gate_ref[strand, at : at + BLOCK, wide]
                for i in range(chunks):
                    chunk = slice(i * CHUNK, (i + 1) * CHUNK)
                    gated = (inside[i] + base_ref[index4, chunk, wide]) * gate[chunk]
                    gated_ref[index4, at + i * CHUNK : at + (i + 1) * CHUNK, wide] = gated
                    part_sum = jnp.sum(gated * gated, axis=1, keepdims=True)
                    square[i] = part_sum if square[i] is None else square[i] + part_sum
            squares.append(jnp.concatenate(square, axis=0))
        squares = squares[::-1] if falls else squares
        scale = lax.rsqrt(jnp.concatenate(squares, axis=0) * (1.0 / inner) + EPSILON)
        scale_ref[index4] = jnp.broadcast_to(scale, (rows, LANES))

    def run(orders):
        live = [one_pass(index4) for index4 in orders]
        while live:
            live = [p for p in live if next(p, live) is not live]

    for orders in ORDERS:
        run(orders)
    for piece in range(rows // CHUNK):
        at = slice(piece * CHUNK, (piece + 1) * CHUNK)
        for tile in range(inner // LANES):
            wide = slice(tile * LANES, (tile + 1) * LANES)
            total = 0.0
            for param in range(2):
                part = sum(
                    gated_ref[k, at, wide] * scale_ref[k, at]
                    for k in range(len(PASSES))
                    if PASSES[k][2] == param
                )
                total = total + part * gain_ref[param : param + 1, wide]
            mixed_ref[at, wide] = total.astype(BF16)


def join_kernel(count, *refs):
    total = sum(count)
    pieces, outs = refs[:total], refs[total : total + len(count)]
    held, (in_sems, out_sems) = refs[total + len(count) : -2], refs[-2:]
    pairs = []
    for n, buffer in zip(count, held):
        at = 0
        for piece in pieces[:n]:
            pairs.append((piece, buffer.at[pl.ds(at, piece.shape[0])]))
            at += piece.shape[0]
        pieces = pieces[n:]
    for copy in start_all(pairs, in_sems):
        copy.wait()
    for copy in start_all(list(zip(held, outs)), out_sems):
        copy.wait()


def join_all(*groups):
    shapes = [
        ((sum(x.shape[0] for x in group), *group[0].shape[1:]), group[0].dtype) for group in groups
    ]
    pieces = [x for group in groups for x in group]
    return pl.pallas_call(
        partial(join_kernel, [len(group) for group in groups]),
        out_shape=[jax.ShapeDtypeStruct(*shape) for shape in shapes],
        in_specs=[pl.BlockSpec(memory_space=pl.ANY)] * len(pieces),
        out_specs=[pl.BlockSpec(memory_space=pl.ANY)] * len(shapes),
        scratch_shapes=[pltpu.VMEM(*shape) for shape in shapes]
        + [pltpu.SemaphoreType.DMA((len(pieces),)), pltpu.SemaphoreType.DMA((len(shapes),))],
        compiler_params=pltpu.CompilerParams(vmem_limit_bytes=4 * 2**20),
        name="join",
    )(*pieces)


def output_kernel(depth, places, flip, here_ref, side_ref, mixed_ref, *refs):
    pieces = refs[: len(places)]
    out_hbm, weight_ref, out_ref, out_sem = refs[-4:]
    here, side = here_ref[0], side_ref[0]
    for piece, masks in zip(pieces, places):
        for k, mask in enumerate(masks):
            row = pl.multiple_of((here ^ mask) * depth, depth)
            weight_ref[pl.ds(row, depth), :] = piece[k]
    rows, columns = out_ref.shape
    lane = pl.multiple_of((side ^ flip) * columns, columns)
    copies = []
    for part in range(rows // LANES):
        at = slice(part * LANES, (part + 1) * LANES)
        out_ref[at] = dot(mixed_ref[at], weight_ref[...]).astype(BF16)
        copies += start_all(
            [(out_ref.at[at], out_hbm.at[pl.ds(part * LANES, LANES), pl.ds(lane, columns)])],
            out_sem.at[pl.ds(part, 1)],
        )
    for copy in copies:
        copy.wait()


def swap(x, axis, mask):
    count = lax.axis_size(axis)
    return lax.ppermute(x, axis, [(i, i ^ mask) for i in range(count)])


def vmem():
    return pl.BlockSpec(memory_space=pltpu.VMEM)


def hbm():
    return pl.BlockSpec(memory_space=pltpu.HBM)


def smem():
    return pl.BlockSpec(memory_space=pltpu.SMEM)


def on_device(
    token_ids,
    complement,
    embedding,
    in_weight,
    step_weight,
    conv_weight,
    conv_bias,
    step_bias,
    decay_rate,
    skip_gain,
    norm_gain,
    out_weight,
):
    genomes, rows = token_ids.shape
    letters, width = embedding.shape
    taps = conv_weight.shape[1]
    heads = step_weight.shape[1]
    inner = norm_gain.shape[1]
    state = (conv_weight.shape[2] - inner) // 2
    count, sides = lax.axis_size("seq"), lax.axis_size("batch")
    here = lax.axis_index("seq").astype(jnp.int32)[None]
    side = lax.axis_index("batch").astype(jnp.int32)[None]
    depth, columns = out_weight.shape

    join = lambda *x: jnp.concatenate(x, axis=0)
    moved = lambda masks, mask: [m ^ mask for m in masks]
    line, line_masks = out_weight[None], [0]
    tokens = token_ids[None]
    token_line = [swap(tokens, "seq", mask) for mask in range(count - 4, 0, -4)]
    mask = count // 2
    while mask > 2:
        arrived = swap(line, "seq", mask)
        if mask == count // 2:
            projected = jnp.dot(embedding, in_weight, preferred_element_type=F32).astype(BF16)
            arrived, token_line, projected = lax.optimization_barrier(
                (arrived, token_line, projected)
            )
            line, token_line = join_all((line, arrived), (tokens, *token_line[::-1]))
            tokens = [token_line] + [swap(token_line, "seq", m) for m in (1, 2, 3)]
        else:
            (line,) = join_all((line, arrived))
        line_masks = line_masks + moved(line_masks, mask)
        mask //= 2
    across_plane = [swap(line, "seq", mask) for mask in (1, 2, 3)]
    places = [line_masks] + [moved(line_masks, mask) for mask in (1, 2, 3)]

    select, last = word_select(letters, taps)
    word_rows = select.shape[0]
    spread = np.repeat(np.eye(heads, dtype=np.float32), inner // heads, axis=1).astype(
        ml_dtypes.bfloat16
    )
    mixed = []
    for genome in range(genomes):
        inputs = (
            *(x[:, genome] for x in tokens),
            spread,
            embedding,
            step_weight.T,
            step_bias,
            decay_rate,
            skip_gain,
            last,
            select,
            conv_weight,
            conv_bias,
            norm_gain,
            projected,
        )
        mixed.append(
            pl.pallas_call(
                partial(mixer_kernel, letters, taps, state, count),
                out_shape=jax.ShapeDtypeStruct((rows, inner), BF16),
                in_specs=[smem(), smem()] + [vmem()] * len(inputs),
                out_specs=vmem(),
                scratch_shapes=[
                    pltpu.VMEM((4, word_rows + 16, inner + LANES), BF16),
                    pltpu.VMEM((2, 32, inner), BF16),
                    pltpu.VMEM((4, 24, inner), F32),
                    pltpu.VMEM((2, LANES, LANES), BF16),
                    pltpu.VMEM((letters**taps, count * rows), BF16),
                    pltpu.VMEM((4 * heads, count * rows), BF16),
                    pltpu.VMEM((4, BLOCK, inner), F32),
                    pltpu.VMEM((4, rows, inner), F32),
                    pltpu.VMEM((2, rows, inner), F32),
                    pltpu.VMEM((4, rows, LANES), F32),
                ],
                compiler_params=pltpu.CompilerParams(vmem_limit_bytes=VMEM_BYTES),
                cost_estimate=pl.CostEstimate(
                    flops=10**10, bytes_accessed=50 * 2**20, transcendentals=2**22
                ),
                name="mixer",
            )(here, complement, *inputs)
        )
    line, across_plane, mixed = lax.optimization_barrier((line, across_plane, mixed))
    pieces = [line, *across_plane]
    sets = [(pieces, 0)]
    mask = 1
    while mask < sides:
        sets = sets + [([swap(x, "batch", mask) for x in found], s ^ mask) for found, s in sets]
        mask *= 2

    def project(found, flip, mixed, out):
        operands = (here, side, mixed, *found) + (() if out is None else (out,))
        return pl.pallas_call(
            partial(output_kernel, depth, places, flip),
            out_shape=jax.ShapeDtypeStruct((rows, columns * sides), BF16),
            in_specs=[smem(), smem()]
            + [vmem()] * (1 + len(found))
            + [hbm()] * (out is not None),
            out_specs=hbm(),
            scratch_shapes=[
                pltpu.VMEM((depth * count, columns), BF16),
                pltpu.VMEM((rows, columns), BF16),
                pltpu.SemaphoreType.DMA((rows // LANES,)),
            ],
            input_output_aliases={} if out is None else {len(operands) - 1: 0},
            compiler_params=pltpu.CompilerParams(vmem_limit_bytes=8 * 2**20),
            cost_estimate=pl.CostEstimate(
                flops=2 * rows * inner * columns, bytes_accessed=2**22, transcendentals=0
            ),
            name="output",
        )(*operands)

    results = []
    for genome in range(genomes):
        out = None
        for found, flip in sets:
            out = project(found, flip, mixed[genome], out)
        results.append(out[None])
    return join(*results) if genomes > 1 else results[0]


def solution(mesh):
    placed = (P("batch", "seq"),) + (P(),) * 10 + (P("seq", "batch"),)
    return jax.shard_map(
        on_device, mesh=mesh, in_specs=placed, out_specs=P("batch", "seq", None), check_vma=False
    )
```

```python
from functools import partial

import jax
import jax.numpy as jnp
import ml_dtypes
import numpy as np
from jax import lax
from jax.experimental import pallas as pl
from jax.experimental.pallas import tpu as pltpu
from jax.sharding import PartitionSpec as P

BLOCK = 256
CHUNK = 64
LANES = 128
WIDE = 256
LOG2E = 1.4426950408889634
EPSILON = 1e-05
ORDERS = ((0, 1), (2, 3))
VMEM_BYTES = 36 * 2**20
F32 = jnp.float32
BF16 = jnp.bfloat16

TN = (((0,), (0,)), ((), ()))
NT = (((1,), (1,)), ((), ()))
NN = (((1,), (0,)), ((), ()))


def dot(a, b, dims=NN):
    return lax.dot_general(a, b, dims, preferred_element_type=F32)


def iota(shape, dim):
    return lax.broadcasted_iota(jnp.int32, shape, dim)


def split3(x):
    high = x.astype(BF16)
    rest = x - high.astype(F32)
    middle = rest.astype(BF16)
    low = (rest - middle.astype(F32)).astype(BF16)
    return high, middle, low


def silu(x):
    return x / (1.0 + jnp.exp(-x))


def word_select(letters, taps):
    part = -(-letters * taps // 16) * 16
    codes = np.arange(letters**taps)
    select = np.zeros((len(codes), 4 * part), np.float32)
    last = np.zeros((len(codes), 32), np.float32)
    for back in range(taps):
        letter = codes // letters**back % letters
        for copy in range(3):
            select[codes, copy * part + (taps - 1 - back) * letters + letter] = 1
    select[:, 3 * part : 3 * part + 3] = 1
    for copy in range(2):
        last[codes, copy * 16 + codes % letters] = 1
    return select.astype(ml_dtypes.bfloat16), last.astype(ml_dtypes.bfloat16)


PASSES = ((False, 0, 0), (False, 1, 1), (True, 0, 1), (True, 1, 0))


def letter_rows(table, letters, rows, complement):
    row = iota((rows, 1), 0) % letters
    picked = row
    if complement is not None:
        picked = jnp.zeros_like(row)
        for letter in range(letters):
            picked = jnp.where(row == letter, complement(letter), picked)
    result = jnp.broadcast_to(table[0:1], (rows, table.shape[1]))
    for letter in range(1, letters):
        result = jnp.where(picked == letter, table[letter : letter + 1], result)
    return result


def pack_split(x, copies):
    return jnp.concatenate(split3(x)[:copies], axis=0)


def start_all(pairs, sems):
    copies = [
        pltpu.make_async_copy(source, target, sems.at[k]) for k, (source, target) in enumerate(pairs)
    ]
    for copy in copies:
        copy.start()
    return copies


def word_index(both, start, size, falls, taps, letters, before_end):
    lanes = both.shape[1]
    codes, scale = None, 1
    for back in range(taps):
        turned = both if back == 0 else pltpu.roll(both, lanes - back if falls else back, 1)
        part = scale * turned[:, start : start + size]
        codes = part if codes is None else codes + part
        scale *= letters
    return jnp.where(before_end < taps - 1, scale + before_end, codes)


def first_words(tokens, letters, taps, part, width):
    row, col = iota((16, width), 0), iota((16, width), 1)
    inner_col = col % part
    found = (col >= 3 * part) & (col < 3 * part + 3)
    for length in range(1, taps):
        for back in range(length):
            want = (taps - 1 - back) * letters + tokens[length - 1 - back]
            found = found | ((row == length - 1) & (col < 3 * part) & (inner_col == want))
    return jnp.where(found & (row < taps - 1), 1.0, 0.0).astype(BF16)


def first_last(tokens, letters, taps):
    row, col = iota((16, 32), 0), iota((16, 32), 1) % 16
    found = jnp.zeros((16, 32), jnp.bool_)
    for length in range(1, taps):
        found = found | ((row == length - 1) & (col == tokens[length - 1]))
    return jnp.where(found, 1.0, 0.0).astype(BF16)


def spread_rows(spread, index, count):
    heads = spread.shape[0]
    stacked = jnp.concatenate([spread] * count, axis=0)
    return jnp.where(iota(stacked.shape, 0) // heads == index, stacked, jnp.zeros_like(stacked))


def mixer_kernel(
    letters,
    taps,
    state,
    count,
    here_ref,
    complement_ref,
    *refs,
):
    token_refs, refs = refs[:4], refs[4:]
    (
        spread_ref,
        embedding_ref,
        step_weight_ref,
        step_bias_ref,
        rate_ref,
        skip_ref,
        last_ref,
        select_ref,
        conv_weight_ref,
        conv_bias_ref,
        gain_ref,
        projected_ref,
        mixed_ref,
        words_ref,
        gates_ref,
        coefs_ref,
        exponent_ref,
        match_ref,
        weight_ref,
        base_ref,
        gated_ref,
        gate_ref,
        scale_ref,
    ) = refs
    here = here_ref[0]
    rows = mixed_ref.shape[0]
    own = rows // BLOCK
    blocks = count * own
    heads, inner = spread_ref.shape
    head = inner // heads
    full = select_ref.shape[0]
    part_rows = select_ref.shape[1] // 4
    first, past = here * own, (here + 1) * own
    chunks = BLOCK // CHUNK
    as_bf16 = lambda mask: jnp.where(mask, 1.0, 0.0).astype(BF16)
    complement = lambda letter: complement_ref[letter]

    tokens16 = jnp.concatenate([ref[...] for ref in token_refs], axis=0).astype(F32).astype(BF16)
    place, target = iota((blocks, count), 1), iota((blocks, count), 0)
    source = here ^ (place % (count // 4) * 4 + place // (count // 4))
    around = jnp.zeros((3 * blocks, BLOCK), F32)
    for part in range(own):
        block = source * own + part
        pick = jnp.concatenate([as_bf16(block == target + k) for k in (-1, 0, 1)], axis=0)
        around = around + dot(pick, tokens16[:, part * BLOCK : (part + 1) * BLOCK])
    around = around.astype(jnp.int32)
    before, middle, after = (around[k * blocks : (k + 1) * blocks] for k in range(3))
    position = iota((blocks, BLOCK), 0) * BLOCK + iota((blocks, BLOCK), 1)
    rise_index = word_index(
        jnp.concatenate([before, middle], axis=1), BLOCK, BLOCK, False, taps, letters, position
    )
    fall_index = word_index(
        jnp.concatenate([middle, after], axis=1),
        0,
        BLOCK,
        True,
        taps,
        letters,
        blocks * BLOCK - 1 - position,
    )
    block_of = iota((blocks, BLOCK), 0)
    middle_word = full // 2
    word = (iota((full + 16, BLOCK), 0) - middle_word).astype(F32).astype(BF16)
    index = jnp.where(block_of < first, rise_index, fall_index) - middle_word
    index = index.astype(F32).astype(BF16)
    one, zero = jnp.ones((), BF16), jnp.zeros((), BF16)
    for block in range(blocks):
        match_ref[:, block * BLOCK : (block + 1) * BLOCK] = jnp.where(
            word[:full] == index[block : block + 1], one, zero
        )
    ends = [
        jnp.where(word[full:] == index[block : block + 1], one, zero) for block in (0, blocks - 1)
    ]

    end_tokens = (
        [middle[:1, k : k + 1] for k in range(taps - 1)],
        [middle[blocks - 1 :, BLOCK - 1 - k : BLOCK - k] for k in range(taps - 1)],
    )

    letter_hot = [jnp.where(middle == letter, 1.0, 0.0) for letter in range(letters)]
    stack = jnp.concatenate(letter_hot, axis=0).astype(BF16)
    t = iota((BLOCK, BLOCK), 0)
    u = iota((BLOCK, BLOCK), 1)
    sums = dot(stack, jnp.concatenate([as_bf16(t <= u), jnp.ones((BLOCK, BLOCK), BF16)], axis=1))
    running, block_sum = sums[:, :BLOCK], sums[:, BLOCK:].astype(BF16)
    col, row = iota((blocks, blocks), 1), iota((blocks, blocks), 0)
    to_rise = as_bf16((col >= row) & (col < first))
    to_fall = as_bf16((col >= past) & (col < row))
    both_ways = jnp.concatenate([to_rise, to_fall], axis=0)
    counts = []
    for letter in range(letters):
        part = slice(letter * blocks, (letter + 1) * blocks)
        far = dot(both_ways, block_sum[part])
        rise = far[:blocks] - running[part]
        fall = far[blocks:] + running[part] - letter_hot[letter]
        counts.append(jnp.where(block_of < first, rise, fall))

    same = (t // CHUNK) == (u // CHUNK)
    until, since = as_bf16(same & (u <= t)), as_bf16(same & (u >= t))
    half = iota((BLOCK, LANES), 1) % CHUNK
    inside_row = iota((BLOCK, LANES), 0) % CHUNK
    lane = iota((BLOCK, LANES), 1)
    hot_lane = jnp.where(lane < 48, (lane % 16).astype(F32), -1.0)
    word_lane = iota((BLOCK, full), 1).astype(F32)
    end_lane = (iota((16, 16), 1) + full).astype(F32)
    small_half = iota((CHUNK, LANES), 1) % CHUNK
    small_row = iota((CHUNK, LANES), 0)
    small_lane = iota((CHUNK, LANES), 1)
    row_lane = iota((1, LANES), 1)
    beyond = (as_bf16(inside_row > half), as_bf16(inside_row < half))
    row8 = iota((8, BLOCK), 0)
    prepared = []
    for part in range(own):
        mine = block_of == first + part
        take = lambda x: jnp.sum(jnp.where(mine, x, 0), axis=0, keepdims=True)
        token_row = take(middle).astype(F32)
        facts = jnp.where(row8 == 0, take(rise_index), take(fall_index)).astype(F32)
        facts = jnp.where(row8 == 2, token_row, facts)
        facts = jnp.concatenate([facts, jnp.zeros((LANES - 8, BLOCK), F32)], axis=0).T
        matches = [
            jnp.where(word_lane == facts[:, d : d + 1], 1.0, 0.0).astype(BF16) for d in range(2)
        ]
        matches += [
            jnp.where(end_lane == facts[at : at + 16, d : d + 1], 1.0, 0.0).astype(BF16)
            for d, at in ((0, 0), (1, BLOCK - 16))
        ]
        hot = jnp.where(hot_lane == facts[:, 2:3], 1.0, 0.0)
        hot16 = hot.astype(BF16)
        tallies = dot(jnp.concatenate([until, since], axis=0), hot16)
        hot_rows = [jnp.where(token_row == l, 1.0, 0.0) for l in range(letters)]
        between = []
        for d, reach in enumerate((until, since)):
            left = jnp.concatenate([reach * h.astype(BF16) for h in hot_rows], axis=0)
            between.append(dot(left, beyond[d]))
        totals = jnp.concatenate(
            [jnp.where(u[:1] // CHUNK == i, h, 0.0) for i in range(chunks) for h in hot_rows],
            axis=0,
        ).astype(BF16)
        totals = dot(totals, jnp.ones((BLOCK, LANES), BF16))
        doubled = []
        for i in range(chunks):
            window = token_row[:, (i // 2) * LANES : (i // 2 + 1) * LANES]
            keep = (row_lane // CHUNK) == i % 2
            doubled.append(jnp.where(keep, window, pltpu.roll(window, CHUNK, 1)))
        prepared.append((matches, hot, hot16, tallies, between, totals, doubled))

    spread = spread_ref[...]
    width = embedding_ref.shape[1]
    embedding = jnp.concatenate(
        [embedding_ref[...], jnp.zeros((16 - letters, width), BF16)], axis=0
    )
    raw = dot(embedding, step_weight_ref[...], NT)

    def widen(x):
        return sum(dot(piece, spread) for piece in split3(x))

    row = iota((16, heads), 0)
    vectors = jnp.zeros((16, heads), F32)
    for k in range(2):
        vectors = jnp.where(row == k, step_bias_ref[k : k + 1, :], vectors)
        vectors = jnp.where(row == 2 + k, rate_ref[k : k + 1, :], vectors)
        vectors = jnp.where(row == 4 + k, skip_ref[k : k + 1, :], vectors)
    wide_both = widen(jnp.concatenate([raw, vectors], axis=0))
    wide_raw, wide_vectors = wide_both[:16], wide_both[16:]

    def step_tables(raw_rows, vector_rows, strand, param):
        rows8 = letter_rows(raw_rows, letters, 8, complement if strand else None)
        shifted = rows8 + vector_rows[param : param + 1]
        step = jnp.maximum(shifted, 0.0) + jnp.log1p(jnp.exp(-jnp.abs(shifted)))
        decay = jnp.maximum(-vector_rows[2 + param : 3 + param] * step * LOG2E, -1e30)
        return step, decay, jnp.maximum(jnp.log2(step), -1000.0)

    lane8 = iota((8, LANES), 1)
    exponents = [jnp.zeros((8, LANES), F32)] * 3
    talls = []
    for index4, (falls, strand, param) in enumerate(PASSES):
        _, decay, log_step = step_tables(wide_raw, wide_vectors, strand, param)
        coefs_ref[index4, 0:8] = decay
        coefs_ref[index4, 8:16] = log_step
        coefs_ref[index4, 16:24] = jnp.broadcast_to(wide_vectors[4 + param : 5 + param], (8, inner))
        step, decay, log_step = step_tables(raw, vectors, strand, param)
        for place, narrow in enumerate((decay, log_step, step)):
            wide = jnp.concatenate([narrow, jnp.zeros((8, LANES - heads), F32)], axis=1)
            wide = pltpu.roll(wide, index4 * heads, 1) if index4 else wide
            mine = (lane8 >= index4 * heads) & (lane8 < (index4 + 1) * heads)
            exponents[place] = jnp.where(mine, wide, exponents[place])
    only = iota((8, LANES), 0) < letters
    tall = jnp.concatenate([exponents[0], jnp.zeros((LANES - 8, LANES), F32)], axis=0).T
    exponents = [
        jnp.concatenate([jnp.where(only, x, 0.0), jnp.zeros((8, LANES), F32)], axis=0)
        for x in exponents
    ]
    for place in range(2):
        rest = jnp.zeros((LANES - 48, LANES), BF16)
        exponent_ref[place] = jnp.concatenate([*split3(exponents[place]), rest], axis=0)
    lasts = [last_ref[...]] + [first_last(x, letters, taps) for x in end_tokens]
    word_steps = dot(jnp.concatenate(lasts, axis=0), pack_split(exponents[2], 2))

    talls = [
        [
            jnp.broadcast_to(tall[k * 2 * heads : (k + 1) * 2 * heads, l : l + 1], (2 * heads, BLOCK))
            for l in range(letters)
        ]
        for k in range(2)
    ]
    for block in range(blocks):
        rises, falls = block < first, block >= past
        power = sum(
            counts[l][block : block + 1] * jnp.where(rises, talls[0][l], talls[1][l])
            for l in range(letters)
        )
        weight = jnp.exp2(power)
        lanes = slice(block * BLOCK, (block + 1) * BLOCK)
        weight_ref[: 2 * heads, lanes] = jnp.where(rises, weight, 0.0).astype(BF16)
        weight_ref[2 * heads :, lanes] = jnp.where(falls, weight, 0.0).astype(BF16)
    word_weights = dot(match_ref[...], weight_ref[...], NT)
    end_weights = [
        dot(end, weight_ref[:, block * BLOCK : (block + 1) * BLOCK], NT)
        for end, block in zip(ends, (0, blocks - 1))
    ]
    word_weights = jnp.concatenate([word_weights, *end_weights], axis=0)
    word_weights = (word_weights * word_steps[:, : 4 * heads]).astype(BF16)
    end_selects = [
        first_words(x, letters, taps, part_rows, 4 * part_rows) for x in end_tokens
    ]

    narrows = []
    for matches, hot, hot16, tallies, between, totals, doubled in prepared:
        up, down = tallies[:BLOCK], tallies[BLOCK:]
        powers = dot(
            jnp.concatenate([up, down, down - hot, up - hot], axis=0).astype(BF16), exponent_ref[0]
        )
        power = lambda k: powers[k * BLOCK : (k + 1) * BLOCK]
        steps = dot(hot16, exponent_ref[1])
        chunk_power = [power(0)[(i + 1) * CHUNK - 1 : (i + 1) * CHUNK] for i in range(chunks)]
        found = []
        for falls in (False, True):
            ends_at = power(2 + falls) + steps
            pieces = [power(int(falls))]
            for i in range(chunks + 1):
                target = chunks - 1 - i if falls else i
                if i == chunks and own == 1:
                    continue
                for j in range(chunks):
                    passed = range(target + 1, j) if falls else range(j + 1, target)
                    if (j > target) if falls else (j < target):
                        pieces.append(
                            ends_at[j * CHUNK : (j + 1) * CHUNK] + sum(chunk_power[m] for m in passed)
                        )
            found.append(jnp.exp2(jnp.concatenate(pieces, axis=0)).astype(BF16)[:, : 4 * heads])
        narrows.append(found)

    projected = projected_ref[...].astype(F32)
    gate = silu(projected[:, :inner])
    for strand in range(2):
        gate_rows = letter_rows(gate, letters, 16, complement if strand else None)
        gate_rows = jnp.where(iota((16, 1), 0) < letters, gate_rows, 0.0)
        gates_ref[strand] = pack_split(gate_rows, 2)

    block_chunk = t // CHUNK
    lane_chunk = u // CHUNK
    head_of = iota((CHUNK, WIDE), 1) // head
    head_masks = [as_bf16(head_of == h) for h in range(WIDE // head)]
    def one_pass(index4):
        falls, strand, param = PASSES[index4]
        d = int(falls)
        inputs = letter_rows(
            projected[:, inner:], letters, part_rows, complement if strand else None
        )
        tap_row = iota((part_rows, 1), 0) // letters
        weights = jnp.zeros((part_rows, inputs.shape[1]), F32)
        for tap in range(taps):
            weights = jnp.where(tap_row == tap, conv_weight_ref[param, tap : tap + 1, :], weights)
        bias_rows = jnp.zeros((part_rows, inputs.shape[1]), F32)
        for place, piece in enumerate(split3(conv_bias_ref[param : param + 1, :])):
            bias_rows = jnp.where(iota((part_rows, 1), 0) == place, piece.astype(F32), bias_rows)
        products = jnp.concatenate([*split3(weights * inputs), bias_rows.astype(BF16)], axis=0)
        select = jnp.concatenate([select_ref[...], end_selects[d]], axis=0)
        conved = silu(dot(select, products))
        yield
        words_ref[index4, :, :inner] = conved[:, :inner].astype(BF16)
        rest = conved[:, inner:]
        rest_lane = iota(rest.shape, 1)
        words_ref[index4, :, inner : inner + LANES] = jnp.where(
            rest_lane < state, pltpu.roll(rest, LANES - state, 1), 0.0
        ).astype(BF16)
        turned = rest.T[:state].astype(BF16)
        to_lanes = spread_rows(spread, index4, 4)
        yield
        own_weights = jnp.concatenate(
            [word_weights[:full], word_weights[full + 16 * d : full + 16 * (d + 1)]], axis=0
        )
        weighted = (dot(own_weights, to_lanes) * conved[:, :inner]).astype(BF16)
        held = dot(turned, weighted)

        yield
        decay = [coefs_ref[index4, l : l + 1] for l in range(letters)]
        log_step = [coefs_ref[index4, 8 + l : 9 + l] for l in range(letters)]
        skip = coefs_ref[index4, 16:17]
        squares = []
        for part in range(own - 1, -1, -1) if falls else range(own):
            matches, _, hot16, _, between, totals, doubled = prepared[part]
            match, end_match, at = matches[d], matches[2 + d], part * BLOCK

            def looked_up(columns):
                found = dot(match, words_ref[index4, :full, columns])
                more = dot(end_match, words_ref[index4, full:, columns])
                if falls:
                    return jnp.concatenate([found[: BLOCK - 16], found[BLOCK - 16 :] + more], axis=0)
                return jnp.concatenate([found[:16] + more, found[16:]], axis=0)

            order = range(chunks - 1, -1, -1) if falls else range(chunks)
            end_bt = dot(turned[:, full:], end_match, NT)
            bt = dot(turned[:, :full], match, NT)
            if falls:
                bt = jnp.concatenate([bt[:, : BLOCK - 16], bt[:, BLOCK - 16 :] + end_bt], axis=1)
            else:
                bt = jnp.concatenate([bt[:, :16] + end_bt, bt[:, 16:]], axis=1)
            c_rows = looked_up(slice(inner, inner + LANES))
            values = looked_up(slice(0, inner))
            yield
            spreads = dot(narrows[part][d], to_lanes)
            yield
            c16, bt16 = c_rows.astype(BF16)[:, :state], bt.astype(BF16)
            all_scores = dot(c16, bt16)
            values16 = values.astype(BF16)
            scores = []
            for i in range(chunks):
                lanes = slice((i // 2) * LANES, (i // 2 + 1) * LANES)
                window = all_scores[i * CHUNK : (i + 1) * CHUNK, lanes]
                keep = (small_lane // CHUNK) == i % 2
                both = jnp.where(keep, window, pltpu.roll(window, CHUNK, 1))
                causal = (small_half >= small_row) if falls else (small_half <= small_row)
                scores.append(jnp.where(causal, both, 0.0))
            yield
            twice = c_rows + pltpu.roll(c_rows, state, 1)
            c_chunks = jnp.concatenate([twice] * (chunks * state // LANES), axis=1)
            earlier = (lane_chunk > block_chunk) if falls else (lane_chunk < block_chunk)
            left = jnp.where(earlier, all_scores, 0.0)
            left = jnp.where(lane_chunk == block_chunk, c_chunks, left).astype(BF16)
            used = BLOCK
            power_sum = None
            pairs = LANES // CHUNK
            for i in order:
                decayed = held if power_sum is None else held * jnp.exp2(power_sum)
                blocks_of = [jnp.zeros((CHUNK, inner), BF16)] * chunks
                blocks_of[i] = decayed.astype(BF16)
                others = range(i + 1, chunks) if falls else range(i)
                for j in others:
                    rows_of = slice(j * CHUNK, (j + 1) * CHUNK)
                    blocks_of[j] = (values[rows_of] * spreads[used : used + CHUNK]).astype(BF16)
                    used += CHUNK
                low = (i // pairs) * pairs if falls else 0
                high = chunks if falls else (i // pairs + 1) * pairs
                chunk = slice(i * CHUNK, (i + 1) * CHUNK)
                carried = dot(
                    left[chunk, low * CHUNK : high * CHUNK],
                    jnp.concatenate(blocks_of[low:high], axis=0),
                )
                base_ref[index4, chunk] = carried * spreads[chunk] + skip * values[chunk]
                for l in range(letters):
                    row = totals[i * letters + l : i * letters + l + 1]
                    row = jnp.concatenate([row] * (inner // LANES), axis=1) * decay[l]
                    power_sum = row if power_sum is None else power_sum + row
            if own > 1:
                fresh = dot(bt16, (values * spreads[used : used + BLOCK]).astype(BF16))
                held = held * jnp.exp2(power_sum) + fresh
            yield
            square = [None] * chunks
            for group in range(inner // WIDE):
                wide = slice(group * WIDE, (group + 1) * WIDE)
                mixed, stacked = [], []
                for i in range(chunks):
                    mixing = []
                    for tile in range(WIDE // LANES):
                        low = group * WIDE + tile * LANES
                        lanes = slice(low, low + LANES)
                        total = log_step[0][:, lanes]
                        for l in range(1, letters):
                            total = jnp.where(doubled[i] == l, log_step[l][:, lanes], total)
                        for l in range(letters):
                            apart = between[d][l * BLOCK + i * CHUNK : l * BLOCK + (i + 1) * CHUNK]
                            total = total + apart * decay[l][:, lanes]
                        mixing.append((jnp.exp2(total) * scores[i]).astype(BF16))
                    mixed.append(jnp.concatenate(mixing, axis=1))
                    chunk_values = values16[i * CHUNK : (i + 1) * CHUNK, wide]
                    stacked.append(
                        jnp.concatenate([chunk_values * mask for mask in head_masks], axis=0)
                    )
                yield
                inside = [dot(m, v) for m, v in zip(mixed, stacked)]
                if index4 == strand:
                    gate_ref[strand, at : at + BLOCK, wide] = dot(
                        hot16[:, :32], gates_ref[strand, :, wide]
                    )
                gate = gate_ref[strand, at : at + BLOCK, wide]
                for i in range(chunks):
                    chunk = slice(i * CHUNK, (i + 1) * CHUNK)
                    gated = (inside[i] + base_ref[index4, chunk, wide]) * gate[chunk]
                    gated_ref[index4, at + i * CHUNK : at + (i + 1) * CHUNK, wide] = gated
                    part_sum = jnp.sum(gated * gated, axis=1, keepdims=True)
                    square[i] = part_sum if square[i] is None else square[i] + part_sum
            squares.append(jnp.concatenate(square, axis=0))
        squares = squares[::-1] if falls else squares
        scale = lax.rsqrt(jnp.concatenate(squares, axis=0) * (1.0 / inner) + EPSILON)
        scale_ref[index4] = jnp.broadcast_to(scale, (rows, LANES))

    def run(orders):
        live = [one_pass(index4) for index4 in orders]
        while live:
            live = [p for p in live if next(p, live) is not live]

    for orders in ORDERS:
        run(orders)
    for piece in range(rows // CHUNK):
        at = slice(piece * CHUNK, (piece + 1) * CHUNK)
        for tile in range(inner // LANES):
            wide = slice(tile * LANES, (tile + 1) * LANES)
            total = 0.0
            for param in range(2):
                part = sum(
                    gated_ref[k, at, wide] * scale_ref[k, at]
                    for k in range(len(PASSES))
                    if PASSES[k][2] == param
                )
                total = total + part * gain_ref[param : param + 1, wide]
            mixed_ref[at, wide] = total.astype(BF16)


def join_kernel(count, *refs):
    total = sum(count)
    pieces, outs = refs[:total], refs[total : total + len(count)]
    held, (in_sems, out_sems) = refs[total + len(count) : -2], refs[-2:]
    pairs = []
    for n, buffer in zip(count, held):
        at = 0
        for piece in pieces[:n]:
            pairs.append((piece, buffer.at[pl.ds(at, piece.shape[0])]))
            at += piece.shape[0]
        pieces = pieces[n:]
    for copy in start_all(pairs, in_sems):
        copy.wait()
    for copy in start_all(list(zip(held, outs)), out_sems):
        copy.wait()


def join_all(*groups):
    shapes = [
        ((sum(x.shape[0] for x in group), *group[0].shape[1:]), group[0].dtype) for group in groups
    ]
    pieces = [x for group in groups for x in group]
    return pl.pallas_call(
        partial(join_kernel, [len(group) for group in groups]),
        out_shape=[jax.ShapeDtypeStruct(*shape) for shape in shapes],
        in_specs=[pl.BlockSpec(memory_space=pl.ANY)] * len(pieces),
        out_specs=[pl.BlockSpec(memory_space=pl.ANY)] * len(shapes),
        scratch_shapes=[pltpu.VMEM(*shape) for shape in shapes]
        + [pltpu.SemaphoreType.DMA((len(pieces),)), pltpu.SemaphoreType.DMA((len(shapes),))],
        compiler_params=pltpu.CompilerParams(vmem_limit_bytes=4 * 2**20),
        name="join",
    )(*pieces)


def output_kernel(depth, places, flip, here_ref, side_ref, mixed_ref, *refs):
    pieces = refs[: len(places)]
    out_hbm, weight_ref, out_ref, out_sem = refs[-4:]
    here, side = here_ref[0], side_ref[0]
    for piece, masks in zip(pieces, places):
        for k, mask in enumerate(masks):
            row = pl.multiple_of((here ^ mask) * depth, depth)
            weight_ref[pl.ds(row, depth), :] = piece[k]
    rows, columns = out_ref.shape
    lane = pl.multiple_of((side ^ flip) * columns, columns)
    copies = []
    for part in range(rows // LANES):
        at = slice(part * LANES, (part + 1) * LANES)
        out_ref[at] = dot(mixed_ref[at], weight_ref[...]).astype(BF16)
        copies += start_all(
            [(out_ref.at[at], out_hbm.at[pl.ds(part * LANES, LANES), pl.ds(lane, columns)])],
            out_sem.at[pl.ds(part, 1)],
        )
    for copy in copies:
        copy.wait()


def swap(x, axis, mask):
    count = lax.axis_size(axis)
    return lax.ppermute(x, axis, [(i, i ^ mask) for i in range(count)])


def vmem():
    return pl.BlockSpec(memory_space=pltpu.VMEM)


def hbm():
    return pl.BlockSpec(memory_space=pltpu.HBM)


def smem():
    return pl.BlockSpec(memory_space=pltpu.SMEM)


def on_device(
    token_ids,
    complement,
    embedding,
    in_weight,
    step_weight,
    conv_weight,
    conv_bias,
    step_bias,
    decay_rate,
    skip_gain,
    norm_gain,
    out_weight,
):
    genomes, rows = token_ids.shape
    letters, width = embedding.shape
    taps = conv_weight.shape[1]
    heads = step_weight.shape[1]
    inner = norm_gain.shape[1]
    state = (conv_weight.shape[2] - inner) // 2
    count, sides = lax.axis_size("seq"), lax.axis_size("batch")
    here = lax.axis_index("seq").astype(jnp.int32)[None]
    side = lax.axis_index("batch").astype(jnp.int32)[None]
    depth, columns = out_weight.shape

    join = lambda *x: jnp.concatenate(x, axis=0)
    moved = lambda masks, mask: [m ^ mask for m in masks]
    line, line_masks = out_weight[None], [0]
    tokens = token_ids[None]
    token_line = [swap(tokens, "seq", mask) for mask in range(count - 4, 0, -4)]
    mask = count // 2
    while mask > 2:
        arrived = swap(line, "seq", mask)
        if mask == count // 2:
            projected = jnp.dot(embedding, in_weight, preferred_element_type=F32).astype(BF16)
            arrived, token_line, projected = lax.optimization_barrier(
                (arrived, token_line, projected)
            )
            line, token_line = join_all((line, arrived), (tokens, *token_line[::-1]))
            tokens = [token_line] + [swap(token_line, "seq", m) for m in (1, 2, 3)]
        else:
            (line,) = join_all((line, arrived))
        line_masks = line_masks + moved(line_masks, mask)
        mask //= 2
    across_plane = [swap(line, "seq", mask) for mask in (1, 2, 3)]
    places = [line_masks] + [moved(line_masks, mask) for mask in (1, 2, 3)]

    select, last = word_select(letters, taps)
    word_rows = select.shape[0]
    spread = np.repeat(np.eye(heads, dtype=np.float32), inner // heads, axis=1).astype(
        ml_dtypes.bfloat16
    )
    mixed = []
    for genome in range(genomes):
        inputs = (
            *(x[:, genome] for x in tokens),
            spread,
            embedding,
            step_weight.T,
            step_bias,
            decay_rate,
            skip_gain,
            last,
            select,
            conv_weight,
            conv_bias,
            norm_gain,
            projected,
        )
        mixed.append(
            pl.pallas_call(
                partial(mixer_kernel, letters, taps, state, count),
                out_shape=jax.ShapeDtypeStruct((rows, inner), BF16),
                in_specs=[smem(), smem()] + [vmem()] * len(inputs),
                out_specs=vmem(),
                scratch_shapes=[
                    pltpu.VMEM((4, word_rows + 16, inner + LANES), BF16),
                    pltpu.VMEM((2, 32, inner), BF16),
                    pltpu.VMEM((4, 24, inner), F32),
                    pltpu.VMEM((2, LANES, LANES), BF16),
                    pltpu.VMEM((letters**taps, count * rows), BF16),
                    pltpu.VMEM((4 * heads, count * rows), BF16),
                    pltpu.VMEM((4, BLOCK, inner), F32),
                    pltpu.VMEM((4, rows, inner), F32),
                    pltpu.VMEM((2, rows, inner), F32),
                    pltpu.VMEM((4, rows, LANES), F32),
                ],
                compiler_params=pltpu.CompilerParams(vmem_limit_bytes=VMEM_BYTES),
                cost_estimate=pl.CostEstimate(
                    flops=10**10, bytes_accessed=50 * 2**20, transcendentals=2**22
                ),
                name="mixer",
            )(here, complement, *inputs)
        )
    line, across_plane, mixed = lax.optimization_barrier((line, across_plane, mixed))
    pieces = [line, *across_plane]
    sets = [(pieces, 0)]
    mask = 1
    while mask < sides:
        sets = sets + [([swap(x, "batch", mask) for x in found], s ^ mask) for found, s in sets]
        mask *= 2

    def project(found, flip, mixed, out):
        operands = (here, side, mixed, *found) + (() if out is None else (out,))
        return pl.pallas_call(
            partial(output_kernel, depth, places, flip),
            out_shape=jax.ShapeDtypeStruct((rows, columns * sides), BF16),
            in_specs=[smem(), smem()]
            + [vmem()] * (1 + len(found))
            + [hbm()] * (out is not None),
            out_specs=hbm(),
            scratch_shapes=[
                pltpu.VMEM((depth * count, columns), BF16),
                pltpu.VMEM((rows, columns), BF16),
                pltpu.SemaphoreType.DMA((rows // LANES,)),
            ],
            input_output_aliases={} if out is None else {len(operands) - 1: 0},
            compiler_params=pltpu.CompilerParams(vmem_limit_bytes=8 * 2**20),
            cost_estimate=pl.CostEstimate(
                flops=2 * rows * inner * columns, bytes_accessed=2**22, transcendentals=0
            ),
            name="output",
        )(*operands)

    results = []
    for genome in range(genomes):
        out = None
        for found, flip in sets:
            out = project(found, flip, mixed[genome], out)
        results.append(out[None])
    return join(*results) if genomes > 1 else results[0]


def solution(mesh):
    placed = (P("batch", "seq"),) + (P(),) * 10 + (P("seq", "batch"),)
    return jax.shard_map(
        on_device, mesh=mesh, in_specs=placed, out_specs=P("batch", "seq", None), check_vma=False
    )
```
